256 devices in a mesh: gx: 64 (over z, x, core), gz: 4 (over y).
Axes of the slice: x: 4, y: 4, z: 8, core: 2. Of those that a mesh axis runs over, the one named last changes fastest.
Arguments:
- velocity: float32 [3, 4096, 32, 256], P(None, 'gx', 'gz'), may hold values from -6 to 6
Outputs:
- smoothed: float32 [9, 4096, 32, 256], P(None, 'gx', 'gz')
- vertical_derivative: float32 [9, 4096, 32, 256], P(None, 'gx', 'gz')
The draws below stay inside these ranges and needn't reach their ends.
All inputs are finite; a program needn't handle non-finite values.
Results may differ from the reference program's by a relative error of at most 0.00014.
Values sent between devices are 32-bit elements; how exact they have to be, the bound alone decides.
A program may use at most 128 MiB of HBM per device.

```python
import jax
import jax.numpy as jnp
from jax import lax

COMP = 3
NY = 256
NX = 4096
NZ = 32


def block_scale(key, dims, shards, least, largest):
    level = 1.0
    for axis_at, parts in shards:
        draws = jax.random.uniform(jax.random.fold_in(jax.random.fold_in(key, 6), axis_at), (parts,), jnp.float32, least / len(shards), largest / len(shards))
        level = level * jnp.repeat(jnp.exp(draws), dims[axis_at] // parts).reshape((-1,) + (1,) * (len(dims) - 1 - axis_at))
    return level


def bell_draw(stream_key, shape, spread, limit, pieces=(), held_as=jnp.bfloat16):
    result = spread * jax.random.normal(stream_key, shape, jnp.float32)
    if pieces:
        result = result * block_scale(stream_key, shape, pieces, -0.22, 0.18)
    return jnp.clip(result, -limit, limit).astype(held_as)


def setup_inputs(seed: int = 0) -> dict:
    arg_keys = jax.random.split(jax.random.key(seed), 2)
    velocity = bell_draw(arg_keys[0], (COMP, NX, NZ, NY), 1.0, 6.0, ((1, 64), (2, 4)), jnp.float32)
    return dict(velocity=velocity)


def products(velocity):
    stream = velocity[0]
    span = velocity[1]
    upward = velocity[2]
    return jnp.stack([stream, span, upward, stream * stream, stream * span, stream * upward, span * span, span * upward, upward * upward])


def reference(velocity):
    fields = products(velocity)

    def shifted(offset):
        return jnp.roll(fields, -offset, axis=2)

    vertical = (45.0 * (shifted(1) - shifted(-1)) - 9.0 * (shifted(2) - shifted(-2)) + (shifted(3) - shifted(-3))) / 60.0
    stiffness = (NX / 8.0) ** 2
    wavenumber = jnp.arange(NX).astype(jnp.float32)
    denominator = 1.0 + 4.0 * stiffness * jnp.sin(jnp.pi * wavenumber / NX) ** 2

    def smooth_one(field):
        spectrum = jnp.fft.fft(field, axis=0)
        return jnp.real(jnp.fft.ifft(spectrum / denominator[:, None, None], axis=0)).astype(field.dtype)

    smoothed = lax.map(smooth_one, fields)
    return smoothed, vertical
```

```python
import functools
import math

import jax
import jax.numpy as jnp
from jax import lax
from jax.experimental import pallas as pl
from jax.experimental.pallas import tpu as pltpu
from jax.sharding import PartitionSpec as P

MESH = pl.DeviceIdType.MESH
F32 = jnp.float32
GROUP = 8
CHUNKS = 8
HALO = 3
DERIV = (45.0 / 60.0, -9.0 / 60.0, 1.0 / 60.0)


def decay_of(stiffness):
    half = 0.5 / math.sqrt(stiffness)
    return math.exp(-2.0 * math.asinh(half)), 1.0 / math.sqrt(1.0 + 4.0 * stiffness)


def fields_of(a, b):
    return (
        a[0],
        a[1],
        a[2],
        a[0] * b[0],
        a[0] * b[1],
        a[0] * b[2],
        a[1] * b[1],
        a[1] * b[2],
        a[2] * b[2],
    )


def by_row(index, values):
    out = jnp.full(index.shape, values[0], F32)
    for i, value in enumerate(values[1:], 1):
        out = jnp.where(index == i, F32(value), out)
    return out


def vertical(center, halo, rows):
    total = None
    for k, coef in enumerate(DERIV, 1):
        upper = [
            pltpu.roll(jnp.where(rows >= k, c, h), 8 - k, 0) for c, h in zip(center, halo)
        ]
        lower = [
            pltpu.roll(jnp.where(rows < 8 - k, c, h), k, 0) for c, h in zip(center, halo)
        ]
        above = fields_of([F32(coef) * a for a in upper], upper)
        below = fields_of([F32(coef) * b for b in lower], lower)
        term = [a - b for a, b in zip(above, below)]
        total = term if total is None else [t + s for t, s in zip(total, term)]
    return total


def exchange_kernel(
    decay,
    scale,
    cells,
    blocks,
    v_hbm,
    local_ref,
    deriv_ref,
    carry_ref,
    v_ref,
    halo_ref,
    sums_ref,
    group_ref,
    total_ref,
    ring_ref,
    scan_ref,
    back_ref,
    load_sem,
    halo_send,
    halo_recv,
    send_sem,
    recv_sem,
):
    me = lax.axis_index("gx")
    y = lax.axis_index("gz")
    y_parts = lax.axis_size("gz")
    ring = blocks // GROUP
    z = me // GROUP
    p = lax.rem(me, GROUP)
    above_id = lax.rem(y + 1, y_parts)
    below_id = lax.rem(y + y_parts - 1, y_parts)
    wide = cells // CHUNKS
    rho = decay**cells
    jump = rho**GROUP

    barrier = pltpu.get_barrier_semaphore()
    for other in (above_id, below_id):
        pl.semaphore_signal(barrier, inc=1, device_id={"gz": other}, device_id_type=MESH)
    for k in range(1, GROUP):
        peer = z * GROUP + lax.rem(p + k, GROUP)
        pl.semaphore_signal(barrier, inc=1, device_id={"gx": peer}, device_id_type=MESH)
    for k in range(1, ring):
        peer = lax.rem(z + k, ring) * GROUP + p
        pl.semaphore_signal(barrier, inc=1, device_id={"gx": peer}, device_id_type=MESH)

    loads = []
    for n in range(CHUNKS):
        part = pl.ds(n * wide, wide)
        loads.append(
            pltpu.make_async_copy(v_hbm.at[:, part], v_ref.at[:, part], load_sem.at[n])
        )
    for load in loads:
        load.start()
    pl.semaphore_wait(barrier, 2 + (GROUP - 1) + (ring - 1))

    halos = []
    for n in range(CHUNKS):
        part = pl.ds(n * wide, wide)
        for side, (first, target) in enumerate(((0, below_id), (8 - HALO, above_id))):
            layers = pl.ds(first, HALO)
            halos.append(
                pltpu.make_async_remote_copy(
                    src_ref=v_hbm.at[:, part, layers],
                    dst_ref=halo_ref.at[:, part, layers],
                    send_sem=halo_send.at[n, side],
                    recv_sem=halo_recv.at[n, side],
                    device_id={"gz": target},
                    device_id_type=MESH,
                )
            )
    for halo in halos:
        halo.start()

    shape = v_ref.shape[2:]
    rows = lax.broadcasted_iota(jnp.int32, shape, 0)
    zero = jnp.zeros(shape, F32)

    def velocity(x):
        return [v_ref[c, x] for c in range(3)]

    def scaled_fields(x):
        v = velocity(x)
        return fields_of([F32(scale) * a for a in v], v)

    def forward(x, state):
        ahead, back, weight = state
        f = scaled_fields(x)
        ahead = tuple(F32(decay) * a + b for a, b in zip(ahead, f))
        back = tuple(a + weight * b for a, b in zip(back, f))
        for i in range(9):
            local_ref[i, x] = ahead[i]
        return ahead, back, weight * F32(decay)

    state = ((zero,) * 9, (zero,) * 9, jnp.ones(shape, F32))
    for n in range(CHUNKS):
        loads[n].wait()

        def some(j, state, n=n):
            for u in range(2):
                state = forward(n * wide + 2 * j + u, state)
            return state

        state = lax.fori_loop(0, wide // 2, some, state)
    for i in range(9):
        sums_ref[i] = state[0][i]
        sums_ref[9 + i] = state[1][i]

    def exchange(stage, source, target, peer_of, source_row, target_row, count):
        copies = []
        for k in range(1, count):
            copies.append(
                pltpu.make_async_remote_copy(
                    src_ref=source.at[:, pl.ds(source_row(k), 1)],
                    dst_ref=target.at[:, pl.ds(target_row, 1)],
                    send_sem=send_sem.at[stage, k],
                    recv_sem=recv_sem.at[stage, k],
                    device_id={"gx": peer_of(k)},
                    device_id_type=MESH,
                )
            )
        for copy in copies:
            copy.start()
        return copies

    def in_group(k):
        return lax.rem(p + k, GROUP)

    def group_peer(k):
        return z * GROUP + in_group(k)

    def ring_peer(k):
        return lax.rem(z + k, ring) * GROUP + p

    first = exchange(0, sums_ref, group_ref, group_peer, in_group, p, GROUP)

    def backward(j, behind):
        x = cells - 1 - j
        for i in range(9):
            local_ref[i, x] = local_ref[i, x] + behind[i]
        f = scaled_fields(x)
        return tuple(F32(decay) * (a + b) for a, b in zip(behind, f))

    def some_back(j, behind):
        for u in range(2):
            behind = backward(2 * j + u, behind)
        return behind

    lax.fori_loop(0, cells // 2, some_back, (zero,) * 9)

    def derive(n):
        halos[2 * n].wait_recv()
        halos[2 * n + 1].wait_recv()

        def one(j, _):
            x = n * wide + j
            out = vertical(velocity(x), [halo_ref[c, x] for c in range(3)], rows)
            for i in range(9):
                deriv_ref[i, x] = out[i]
            return 0

        lax.fori_loop(0, wide, one, 0)

    for copy in first:
        copy.wait_recv()
    ahead_weight = by_row(rows, [rho ** (GROUP - 1 - b) for b in range(GROUP)])
    back_weight = by_row(rows, [rho**b for b in range(GROUP)])
    mine = rows == p
    for i in range(18):
        held = jnp.where(mine, sums_ref[i], group_ref[i])
        group_ref[i] = held
        part = held * (ahead_weight if i < 9 else back_weight)
        total_ref[i] = jnp.broadcast_to(jnp.sum(part, axis=0, keepdims=True), shape)

    second = exchange(1, total_ref, ring_ref, ring_peer, lambda k: z, z, ring)

    for n in range(0, 2):
        derive(n)

    for copy in second:
        copy.wait_recv()
    closed = 1.0 / (1.0 - jump**ring)
    powers = [closed * jump**e for e in range(ring)]
    ahead_weight = by_row(lax.rem(z - rows + 2 * ring - 1, ring), powers)
    back_weight = by_row(lax.rem(rows - z + 2 * ring - 1, ring), powers)
    own = rows == z
    for i in range(18):
        held = jnp.where(own, total_ref[i], ring_ref[i])
        part = held * (ahead_weight if i < 9 else back_weight)
        entering = jnp.broadcast_to(jnp.sum(part, axis=0, keepdims=True), shape)
        if i < 9:
            run = jnp.where(rows == 0, entering, pltpu.roll(group_ref[i], 1, 0))
            for s in (1, 2, 4):
                moved = jnp.where(rows >= s, pltpu.roll(run, s, 0), F32(0))
                run = run + F32(rho**s) * moved
        else:
            run = jnp.where(rows == 7, entering, pltpu.roll(group_ref[i], 7, 0))
            for s in (1, 2, 4):
                moved = jnp.where(rows < 8 - s, pltpu.roll(run, 8 - s, 0), F32(0))
                run = run + F32(rho**s) * moved
        scan_ref[i] = run

    third = exchange(2, scan_ref, back_ref, group_peer, in_group, p, GROUP)

    for n in range(2, 5):
        derive(n)

    for copy in third:
        copy.wait_recv()
    for i in range(18):
        carry_ref[i] = jnp.where(mine, scan_ref[i], back_ref[i])

    for n in range(5, CHUNKS):
        derive(n)
    for copy in halos + first + second + third:
        copy.wait_send()


def write_kernel(decay, cells, local_ref, deriv_ref, carry_ref, out_s, out_d, held, sem_s, sem_d):
    wide = cells // CHUNKS
    copies = []
    for n in range(CHUNKS):
        part = pl.ds(n * wide, wide)
        copies.append(
            pltpu.make_async_copy(deriv_ref.at[:, part], out_d.at[:, part], sem_d.at[n])
        )
    for copy in copies:
        copy.start()
    ahead = [carry_ref[i] for i in range(9)]
    back = [carry_ref[9 + i] for i in range(9)]
    for n in range(CHUNKS):
        part = pl.ds(n * wide, wide)
        for x in range(n * wide, (n + 1) * wide):
            for i in range(9):
                held[i, x] = local_ref[i, x] + (
                    F32(decay ** (x + 1)) * ahead[i] + F32(decay ** (cells - x)) * back[i]
                )
        copy = pltpu.make_async_copy(held.at[:, part], out_s.at[:, part], sem_s.at[n])
        copy.start()
        copies.append(copy)
    for copy in copies:
        copy.wait()


def shards(velocity):
    comps, cells, layers, span = velocity.shape
    blocks = lax.axis_size("gx")
    ring = blocks // GROUP
    decay, scale = decay_of((cells * blocks / 8.0) ** 2)
    big = (9, cells, layers, span)
    small = (18, layers, span)
    local, deriv, carry = pl.pallas_call(
        functools.partial(exchange_kernel, decay, scale, cells, blocks),
        out_shape=(
            pltpu.VMEM(big, F32),
            pltpu.VMEM(big, F32),
            pltpu.VMEM(small, F32),
        ),
        in_specs=[pl.BlockSpec(memory_space=pl.ANY)],
        out_specs=[pl.BlockSpec(memory_space=pltpu.VMEM)] * 3,
        scratch_shapes=[
            pltpu.VMEM((comps, cells, layers, span), F32),
            pltpu.VMEM((comps, cells, layers, span), F32),
        ]
        + [pltpu.VMEM(small, F32)] * 6
        + [
            pltpu.SemaphoreType.DMA((CHUNKS,)),
            pltpu.SemaphoreType.DMA((CHUNKS, 2)),
            pltpu.SemaphoreType.DMA((CHUNKS, 2)),
            pltpu.SemaphoreType.DMA((3, GROUP)),
            pltpu.SemaphoreType.DMA((3, GROUP)),
        ],
        compiler_params=pltpu.CompilerParams(
            collective_id=0, has_side_effects=True, vmem_limit_bytes=24 << 20
        ),
        name="exchange",
    )(velocity)
    return pl.pallas_call(
        functools.partial(write_kernel, decay, cells),
        out_shape=(jax.ShapeDtypeStruct(big, F32), jax.ShapeDtypeStruct(big, F32)),
        in_specs=[pl.BlockSpec(memory_space=pltpu.VMEM)] * 3,
        out_specs=[pl.BlockSpec(memory_space=pltpu.HBM)] * 2,
        scratch_shapes=[
            pltpu.VMEM(big, F32),
            pltpu.SemaphoreType.DMA((CHUNKS,)),
            pltpu.SemaphoreType.DMA((CHUNKS,)),
        ],
        compiler_params=pltpu.CompilerParams(vmem_limit_bytes=24 << 20),
        name="write",
    )(local, deriv, carry)


def solution(mesh):
    spec = P(None, "gx", "gz", None)
    return jax.shard_map(
        shards, mesh=mesh, in_specs=(spec,), out_specs=(spec, spec), check_vma=False
    )
```

```python
import functools
import math

import jax
import jax.numpy as jnp
from jax import lax
from jax.experimental import pallas as pl
from jax.experimental.pallas import tpu as pltpu
from jax.sharding import PartitionSpec as P

MESH = pl.DeviceIdType.MESH
F32 = jnp.float32
GROUP = 8
CHUNKS = 8
HALO = 3
DERIV = (45.0 / 60.0, -9.0 / 60.0, 1.0 / 60.0)


def decay_of(stiffness):
    half = 0.5 / math.sqrt(stiffness)
    return math.exp(-2.0 * math.asinh(half)), 1.0 / math.sqrt(1.0 + 4.0 * stiffness)


def fields_of(a, b):
    return (
        a[0],
        a[1],
        a[2],
        a[0] * b[0],
        a[0] * b[1],
        a[0] * b[2],
        a[1] * b[1],
        a[1] * b[2],
        a[2] * b[2],
    )


def by_row(index, values):
    out = jnp.full(index.shape, values[0], F32)
    for i, value in enumerate(values[1:], 1):
        out = jnp.where(index == i, F32(value), out)
    return out


def vertical(center, halo, rows):
    total = None
    for k, coef in enumerate(DERIV, 1):
        upper = [
            pltpu.roll(jnp.where(rows >= k, c, h), 8 - k, 0) for c, h in zip(center, halo)
        ]
        lower = [
            pltpu.roll(jnp.where(rows < 8 - k, c, h), k, 0) for c, h in zip(center, halo)
        ]
        above = fields_of([F32(coef) * a for a in upper], upper)
        below = fields_of([F32(coef) * b for b in lower], lower)
        term = [a - b for a, b in zip(above, below)]
        total = term if total is None else [t + s for t, s in zip(total, term)]
    return total


def exchange_kernel(
    decay,
    scale,
    cells,
    blocks,
    v_hbm,
    local_ref,
    deriv_ref,
    carry_ref,
    v_ref,
    halo_ref,
    sums_ref,
    group_ref,
    total_ref,
    ring_ref,
    scan_ref,
    back_ref,
    load_sem,
    halo_send,
    halo_recv,
    send_sem,
    recv_sem,
    group_go,
    y_go,
    z_go,
):
    me = lax.axis_index("gx")
    y = lax.axis_index("gz")
    y_parts = lax.axis_size("gz")
    ring = blocks // GROUP
    z = me // GROUP
    p = lax.rem(me, GROUP)
    above_id = lax.rem(y + 1, y_parts)
    below_id = lax.rem(y + y_parts - 1, y_parts)
    wide = cells // CHUNKS
    rho = decay**cells
    jump = rho**GROUP

    def signal(sem, **device):
        pl.semaphore_signal(sem, inc=1, device_id=device, device_id_type=MESH)

    def in_group(k):
        return lax.rem(p + k, GROUP)

    def group_peer(k):
        return z * GROUP + in_group(k)

    def ring_peer(k):
        return lax.rem(z + k, ring) * GROUP + p

    barrier = pltpu.get_barrier_semaphore()
    even = lax.rem(p, 2) == 0
    for k in range(1, GROUP):

        @pl.when(lax.rem(p + k, 2) == 0)
        def _(k=k):
            signal(barrier, gx=group_peer(k))

    def load(n):
        part = pl.ds(n * wide, wide)
        return pltpu.make_async_copy(v_hbm.at[:, part], v_ref.at[:, part], load_sem.at[n])

    for n in range(CHUNKS):
        load(n).start()

    def halo(n, side):
        first, target = ((0, below_id), (8 - HALO, above_id))[side]
        part = pl.ds(n * wide, wide)
        layers = pl.ds(first, HALO)
        return pltpu.make_async_remote_copy(
            src_ref=v_hbm.at[:, part, layers],
            dst_ref=halo_ref.at[:, part, layers],
            send_sem=halo_send.at[n, side],
            recv_sem=halo_recv.at[n, side],
            device_id={"gz": target},
            device_id_type=MESH,
        )

    shape = v_ref.shape[2:]
    rows = lax.broadcasted_iota(jnp.int32, shape, 0)
    zero = jnp.zeros(shape, F32)

    def velocity(x):
        return [v_ref[c, x] for c in range(3)]

    def scaled_fields(x):
        v = velocity(x)
        return fields_of([F32(scale) * a for a in v], v)

    def forward(n, state):
        load(n).wait()
        ahead, back, weight = state
        for u in range(wide):
            x = n * wide + u
            f = scaled_fields(x)
            ahead = [F32(decay) * a + b for a, b in zip(ahead, f)]
            back = [a + weight * b for a, b in zip(back, f)]
            weight = weight * F32(decay)
            for i in range(9):
                local_ref[i, x] = ahead[i]
        return tuple(ahead), tuple(back), weight

    state = ((zero,) * 9, (zero,) * 9, jnp.ones(shape, F32))
    state = lax.fori_loop(0, CHUNKS, forward, state)
    for i in range(9):
        sums_ref[i] = state[0][i]
        sums_ref[9 + i] = state[1][i]

    def exchange(stage, source, target, peer_of, source_row, target_row, order):
        copies = []
        for k in order:
            copies.append(
                pltpu.make_async_remote_copy(
                    src_ref=source.at[:, pl.ds(source_row(k), 1)],
                    dst_ref=target.at[:, pl.ds(target_row, 1)],
                    send_sem=send_sem.at[stage, k],
                    recv_sem=recv_sem.at[stage, k],
                    device_id={"gx": peer_of(k)},
                    device_id_type=MESH,
                )
            )
        for copy in copies:
            copy.start()
        return copies

    group_order = range(1, GROUP)
    ring_order = sorted(range(1, ring), key=lambda k: -min(k, ring - k))

    @pl.when(even)
    def _():
        pl.semaphore_wait(barrier, GROUP - 1)
        signal(group_go, gx=me + 1)

    @pl.when(jnp.logical_not(even))
    def _():
        pl.semaphore_wait(group_go, 1)

    first = exchange(0, sums_ref, group_ref, group_peer, in_group, p, group_order)

    @pl.when(p == 0)
    def _():
        for other in (above_id, below_id):
            signal(barrier, gx=me + 1, gz=other)

    @pl.when(p == 2)
    def _():
        for k in range(1, ring):
            signal(barrier, gx=ring_peer(k) + 1)

    def backward(n, behind):
        for u in range(wide):
            x = cells - 1 - (n * wide + u)
            for i in range(9):
                local_ref[i, x] = local_ref[i, x] + behind[i]
            f = scaled_fields(x)
            behind = [F32(decay) * (a + b) for a, b in zip(behind, f)]
        return tuple(behind)

    lax.fori_loop(0, CHUNKS, backward, (zero,) * 9)

    def gather(collector, count, go):
        @pl.when(p == collector)
        def _():
            pl.semaphore_wait(barrier, count)
            for k in range(1, GROUP):
                signal(go, gx=group_peer(k))

        @pl.when(p != collector)
        def _():
            pl.semaphore_wait(go, 1)

    gather(1, 2, y_go)
    for n in range(CHUNKS):
        for side in range(2):
            halo(n, side).start()

    def derive(n, _):
        halo(n, 0).wait_recv()
        halo(n, 1).wait_recv()

        def one(j, _):
            x = n * wide + j
            out = vertical(velocity(x), [halo_ref[c, x] for c in range(3)], rows)
            for i in range(9):
                deriv_ref[i, x] = out[i]
            return 0

        return lax.fori_loop(0, wide, one, 0)

    rising = by_row(rows, [rho**b for b in range(GROUP)])
    sinking = by_row(rows, [rho ** (GROUP - 1 - b) for b in range(GROUP)])
    mine = rows == p
    for copy in first:
        copy.wait_recv()
    for i in range(18):
        held = jnp.where(mine, sums_ref[i], group_ref[i])
        group_ref[i] = held
        part = held * (sinking if i < 9 else rising)
        total_ref[i] = jnp.broadcast_to(jnp.sum(part, axis=0, keepdims=True), shape)

    gather(3, ring - 1, z_go)
    second = exchange(1, total_ref, ring_ref, ring_peer, lambda k: z, z, ring_order)

    for i in range(18):
        if i < 9:
            run = jnp.where(rows >= 1, pltpu.roll(group_ref[i], 1, 0), F32(0))
            for s in (1, 2, 4):
                moved = jnp.where(rows >= s, pltpu.roll(run, s, 0), F32(0))
                run = run + F32(rho**s) * moved
        else:
            run = jnp.where(rows < 7, pltpu.roll(group_ref[i], 7, 0), F32(0))
            for s in (1, 2, 4):
                moved = jnp.where(rows < 8 - s, pltpu.roll(run, 8 - s, 0), F32(0))
                run = run + F32(rho**s) * moved
        scan_ref[i] = run

    closed = 1.0 / (1.0 - jump**ring)
    powers = [closed * jump**e for e in range(ring)]
    ahead_weight = by_row(lax.rem(z - rows + 2 * ring - 1, ring), powers)
    back_weight = by_row(lax.rem(rows - z + 2 * ring - 1, ring), powers)
    own = rows == z
    for copy in second:
        copy.wait_recv()
    for i in range(18):
        held = jnp.where(own, total_ref[i], ring_ref[i])
        part = held * (ahead_weight if i < 9 else back_weight)
        entering = jnp.broadcast_to(jnp.sum(part, axis=0, keepdims=True), shape)
        scan_ref[i] = scan_ref[i] + (rising if i < 9 else sinking) * entering

    third = exchange(2, scan_ref, back_ref, group_peer, in_group, p, group_order)

    lax.fori_loop(0, CHUNKS, derive, 0)

    for copy in third:
        copy.wait_recv()
    for i in range(18):
        carry_ref[i] = jnp.where(mine, scan_ref[i], back_ref[i])

    for copy in first + second + third:
        copy.wait_send()
    for n in range(CHUNKS):
        for side in range(2):
            halo(n, side).wait_send()


def write_kernel(decay, cells, local_ref, deriv_ref, carry_ref, out_s, out_d, held, sem_s, sem_d):
    wide = cells // CHUNKS

    def put_d(n):
        part = pl.ds(n * wide, wide)
        return pltpu.make_async_copy(deriv_ref.at[:, part], out_d.at[:, part], sem_d.at[n])

    def put_s(n):
        part = pl.ds(n * wide, wide)
        return pltpu.make_async_copy(held.at[:, part], out_s.at[:, part], sem_s.at[n])

    for n in range(CHUNKS):
        put_d(n).start()

    def correct(n, weights):
        rising, falling = weights
        for u in range(wide):
            x = n * wide + u
            up = rising * F32(decay ** (u + 1))
            down = falling * F32(decay ** (wide - u))
            for i in range(9):
                held[i, x] = local_ref[i, x] + (up * carry_ref[i] + down * carry_ref[9 + i])
        put_s(n).start()
        return rising * F32(decay**wide), falling * F32(decay**-wide)

    shape = carry_ref.shape[1:]
    ones = jnp.ones(shape, F32)
    lax.fori_loop(0, CHUNKS, correct, (ones, ones * F32(decay ** (cells - wide))))
    for n in range(CHUNKS):
        put_d(n).wait()
        put_s(n).wait()


def shards(velocity):
    comps, cells, layers, span = velocity.shape
    blocks = lax.axis_size("gx")
    ring = blocks // GROUP
    decay, scale = decay_of((cells * blocks / 8.0) ** 2)
    big = (9, cells, layers, span)
    small = (18, layers, span)
    local, deriv, carry = pl.pallas_call(
        functools.partial(exchange_kernel, decay, scale, cells, blocks),
        out_shape=(
            pltpu.VMEM(big, F32),
            pltpu.VMEM(big, F32),
            pltpu.VMEM(small, F32),
        ),
        in_specs=[pl.BlockSpec(memory_space=pl.ANY)],
        out_specs=[pl.BlockSpec(memory_space=pltpu.VMEM)] * 3,
        scratch_shapes=[
            pltpu.VMEM((comps, cells, layers, span), F32),
            pltpu.VMEM((comps, cells, layers, span), F32),
        ]
        + [pltpu.VMEM(small, F32)] * 6
        + [
            pltpu.SemaphoreType.DMA((CHUNKS,)),
            pltpu.SemaphoreType.DMA((CHUNKS, 2)),
            pltpu.SemaphoreType.DMA((CHUNKS, 2)),
            pltpu.SemaphoreType.DMA((3, GROUP)),
            pltpu.SemaphoreType.DMA((3, GROUP)),
            pltpu.SemaphoreType.REGULAR,
            pltpu.SemaphoreType.REGULAR,
            pltpu.SemaphoreType.REGULAR,
        ],
        compiler_params=pltpu.CompilerParams(
            collective_id=0, has_side_effects=True, vmem_limit_bytes=44 << 20
        ),
        name="exchange",
    )(velocity)
    return pl.pallas_call(
        functools.partial(write_kernel, decay, cells),
        out_shape=(jax.ShapeDtypeStruct(big, F32), jax.ShapeDtypeStruct(big, F32)),
        in_specs=[pl.BlockSpec(memory_space=pltpu.VMEM)] * 3,
        out_specs=[pl.BlockSpec(memory_space=pltpu.HBM)] * 2,
        scratch_shapes=[
            pltpu.VMEM(big, F32),
            pltpu.SemaphoreType.DMA((CHUNKS,)),
            pltpu.SemaphoreType.DMA((CHUNKS,)),
        ],
        compiler_params=pltpu.CompilerParams(vmem_limit_bytes=24 << 20),
        name="write",
    )(local, deriv, carry)


def solution(mesh):
    spec = P(None, "gx", "gz", None)
    return jax.shard_map(
        shards, mesh=mesh, in_specs=(spec,), out_specs=(spec, spec), check_vma=False
    )
```

```python
import functools
import math

import jax
import jax.numpy as jnp
from jax import lax
from jax.experimental import pallas as pl
from jax.experimental.pallas import tpu as pltpu
from jax.sharding import PartitionSpec as P

MESH = pl.DeviceIdType.MESH
F32 = jnp.float32
GROUP = 8
CHUNKS = 8
HALO = 3
DERIV = (45.0 / 60.0, -9.0 / 60.0, 1.0 / 60.0)


def decay_of(stiffness):
    half = 0.5 / math.sqrt(stiffness)
    return math.exp(-2.0 * math.asinh(half)), 1.0 / math.sqrt(1.0 + 4.0 * stiffness)


def fields_of(a, b):
    return (
        a[0],
        a[1],
        a[2],
        a[0] * b[0],
        a[0] * b[1],
        a[0] * b[2],
        a[1] * b[1],
        a[1] * b[2],
        a[2] * b[2],
    )


def by_row(index, values):
    out = jnp.full(index.shape, values[0], F32)
    for i, value in enumerate(values[1:], 1):
        out = jnp.where(index == i, F32(value), out)
    return out


def vertical(center, halo, rows):
    total = None
    for k, coef in enumerate(DERIV, 1):
        upper = [
            pltpu.roll(jnp.where(rows >= k, c, h), 8 - k, 0) for c, h in zip(center, halo)
        ]
        lower = [
            pltpu.roll(jnp.where(rows < 8 - k, c, h), k, 0) for c, h in zip(center, halo)
        ]
        above = fields_of([F32(coef) * a for a in upper], upper)
        below = fields_of([F32(coef) * b for b in lower], lower)
        term = [a - b for a, b in zip(above, below)]
        total = term if total is None else [t + s for t, s in zip(total, term)]
    return total


def exchange_kernel(
    decay,
    scale,
    cells,
    blocks,
    v_hbm,
    local_ref,
    deriv_ref,
    carry_ref,
    v_ref,
    halo_ref,
    sums_ref,
    group_ref,
    total_ref,
    ring_ref,
    scan_ref,
    back_ref,
    load_sem,
    halo_send,
    halo_recv,
    send_sem,
    recv_sem,
    group_go,
    y_go,
    z_go,
):
    me = lax.axis_index("gx")
    y = lax.axis_index("gz")
    y_parts = lax.axis_size("gz")
    ring = blocks // GROUP
    z = me // GROUP
    p = lax.rem(me, GROUP)
    above_id = lax.rem(y + 1, y_parts)
    below_id = lax.rem(y + y_parts - 1, y_parts)
    wide = cells // CHUNKS
    rho = decay**cells
    jump = rho**GROUP

    def signal(sem, **device):
        pl.semaphore_signal(sem, inc=1, device_id=device, device_id_type=MESH)

    def in_group(k):
        return lax.rem(p + k, GROUP)

    def group_peer(k):
        return z * GROUP + in_group(k)

    def ring_peer(k):
        return lax.rem(z + k, ring) * GROUP + p

    barrier = pltpu.get_barrier_semaphore()
    even = lax.rem(p, 2) == 0
    for k in range(1, GROUP):

        @pl.when(lax.rem(p + k, 2) == 0)
        def _(k=k):
            signal(barrier, gx=group_peer(k))

    second_chip = p // 2 == 1
    for other in (above_id, below_id):

        @pl.when(second_chip)
        def _(other=other):
            signal(barrier, gx=z * GROUP + 1, gz=other)

        @pl.when(jnp.logical_not(second_chip))
        def _(other=other):
            signal(barrier, gx=me + 1 - lax.rem(p, 2), gz=other)

    def load(n):
        part = pl.ds(n * wide, wide)
        return pltpu.make_async_copy(v_hbm.at[:, part], v_ref.at[:, part], load_sem.at[n])

    for n in range(CHUNKS):
        load(n).start()

    def halo(n, side):
        first, target = ((0, below_id), (8 - HALO, above_id))[side]
        part = pl.ds(n * wide, wide)
        layers = pl.ds(first, HALO)
        return pltpu.make_async_remote_copy(
            src_ref=v_hbm.at[:, part, layers],
            dst_ref=halo_ref.at[:, part, layers],
            send_sem=halo_send.at[n, side],
            recv_sem=halo_recv.at[n, side],
            device_id={"gz": target},
            device_id_type=MESH,
        )

    shape = v_ref.shape[2:]
    rows = lax.broadcasted_iota(jnp.int32, shape, 0)
    zero = jnp.zeros(shape, F32)

    def velocity(x):
        return [v_ref[c, x] for c in range(3)]

    def scaled_fields(x):
        v = velocity(x)
        return fields_of([F32(scale) * a for a in v], v)

    def forward(n, state):
        load(n).wait()
        ahead, back, weight = state
        for u in range(wide):
            x = n * wide + u
            f = scaled_fields(x)
            ahead = [F32(decay) * a + b for a, b in zip(ahead, f)]
            back = [a + weight * b for a, b in zip(back, f)]
            weight = weight * F32(decay)
            for i in range(9):
                local_ref[i, x] = ahead[i]
        return tuple(ahead), tuple(back), weight

    state = ((zero,) * 9, (zero,) * 9, jnp.ones(shape, F32))
    state = lax.fori_loop(0, CHUNKS, forward, state)
    for i in range(9):
        sums_ref[i] = state[0][i]
        sums_ref[9 + i] = state[1][i]

    def exchange(stage, source, target, peer_of, source_row, target_row, order):
        copies = []
        for k in order:
            copies.append(
                pltpu.make_async_remote_copy(
                    src_ref=source.at[:, pl.ds(source_row(k), 1)],
                    dst_ref=target.at[:, pl.ds(target_row, 1)],
                    send_sem=send_sem.at[stage, k],
                    recv_sem=recv_sem.at[stage, k],
                    device_id={"gx": peer_of(k)},
                    device_id_type=MESH,
                )
            )
        for copy in copies:
            copy.start()
        return copies

    group_order = sorted(range(1, GROUP), key=lambda k: abs(k - GROUP // 2))

    @pl.when(even)
    def _():
        pl.semaphore_wait(barrier, GROUP - 1)
        signal(group_go, gx=me + 1)

    @pl.when(jnp.logical_not(even))
    def _():
        pl.semaphore_wait(group_go, 1)

    @pl.when(p == 2)
    def _():
        for k in range(1, ring):
            signal(barrier, gx=ring_peer(k) + 1)

    first = exchange(0, sums_ref, group_ref, group_peer, in_group, p, group_order)

    @pl.when(p == 1)
    def _():
        pl.semaphore_wait(barrier, 8)
        for target in (me - 1, me + 1, me + 2):
            signal(y_go, gx=target)

    @pl.when(jnp.logical_and(jnp.logical_not(even), p >= 5))
    def _():
        pl.semaphore_wait(barrier, 4)
        signal(y_go, gx=me - 1)

    @pl.when(jnp.logical_or(even, p == 3))
    def _():
        pl.semaphore_wait(y_go, 1)

    for n in range(CHUNKS):
        for side in range(2):
            halo(n, side).start()

    def backward(n, behind):
        for u in range(wide):
            x = cells - 1 - (n * wide + u)
            for i in range(9):
                local_ref[i, x] = local_ref[i, x] + behind[i]
            f = scaled_fields(x)
            behind = [F32(decay) * (a + b) for a, b in zip(behind, f)]
        return tuple(behind)

    lax.fori_loop(0, CHUNKS, backward, (zero,) * 9)

    @pl.when(p == 3)
    def _():
        pl.semaphore_wait(barrier, ring - 1)
        for k in range(1, GROUP):
            signal(z_go, gx=group_peer(k))

    def derive(n, _):
        halo(n, 0).wait_recv()
        halo(n, 1).wait_recv()

        def one(j, _):
            x = n * wide + j
            out = vertical(velocity(x), [halo_ref[c, x] for c in range(3)], rows)
            for i in range(9):
                deriv_ref[i, x] = out[i]
            return 0

        return lax.fori_loop(0, wide, one, 0)

    rising = by_row(rows, [rho**b for b in range(GROUP)])
    sinking = by_row(rows, [rho ** (GROUP - 1 - b) for b in range(GROUP)])
    mine = rows == p
    for copy in first:
        copy.wait_recv()
    for i in range(18):
        held = jnp.where(mine, sums_ref[i], group_ref[i])
        group_ref[i] = held
        part = held * (sinking if i < 9 else rising)
        total_ref[i] = jnp.broadcast_to(jnp.sum(part, axis=0, keepdims=True), shape)

    @pl.when(p != 3)
    def _():
        pl.semaphore_wait(z_go, 1)

    def total_copy(target, sent, received):
        return pltpu.make_async_remote_copy(
            src_ref=total_ref.at[:, pl.ds(z, 1)],
            dst_ref=ring_ref.at[:, pl.ds(z, 1)],
            send_sem=send_sem.at[1, sent],
            recv_sem=recv_sem.at[1, received],
            device_id={"gx": target * GROUP + p},
            device_id_type=MESH,
        )

    second = [total_copy(0, j, j) for j in range(ring - 1)]
    for j in range(ring - 1):
        target = j + (j + ring - z) // ring
        total_copy(target, j, z - 1 + (target + ring - z) // ring).start()

    for i in range(18):
        if i < 9:
            run = jnp.where(rows >= 1, pltpu.roll(group_ref[i], 1, 0), F32(0))
            for s in (1, 2, 4):
                moved = jnp.where(rows >= s, pltpu.roll(run, s, 0), F32(0))
                run = run + F32(rho**s) * moved
        else:
            run = jnp.where(rows < 7, pltpu.roll(group_ref[i], 7, 0), F32(0))
            for s in (1, 2, 4):
                moved = jnp.where(rows < 8 - s, pltpu.roll(run, 8 - s, 0), F32(0))
                run = run + F32(rho**s) * moved
        scan_ref[i] = run

    closed = 1.0 / (1.0 - jump**ring)
    powers = [closed * jump**e for e in range(ring)]
    ahead_weight = by_row(lax.rem(z - rows + 2 * ring - 1, ring), powers)
    back_weight = by_row(lax.rem(rows - z + 2 * ring - 1, ring), powers)
    own = rows == z
    for copy in second:
        copy.wait_recv()
    for i in range(18):
        held = jnp.where(own, total_ref[i], ring_ref[i])
        part = held * (ahead_weight if i < 9 else back_weight)
        entering = jnp.broadcast_to(jnp.sum(part, axis=0, keepdims=True), shape)
        scan_ref[i] = scan_ref[i] + (rising if i < 9 else sinking) * entering

    third = exchange(2, scan_ref, back_ref, group_peer, in_group, p, group_order)

    lax.fori_loop(0, CHUNKS, derive, 0)

    for copy in third:
        copy.wait_recv()
    for i in range(18):
        carry_ref[i] = jnp.where(mine, scan_ref[i], back_ref[i])

    for copy in first + second + third:
        copy.wait_send()
    for n in range(CHUNKS):
        for side in range(2):
            halo(n, side).wait_send()


def write_kernel(decay, cells, local_ref, deriv_ref, carry_ref, out_s, out_d, held, sem_s, sem_d):
    wide = cells // CHUNKS

    def put_d(n):
        part = pl.ds(n * wide, wide)
        return pltpu.make_async_copy(deriv_ref.at[:, part], out_d.at[:, part], sem_d.at[n])

    def put_s(n):
        part = pl.ds(n * wide, wide)
        return pltpu.make_async_copy(held.at[:, part], out_s.at[:, part], sem_s.at[n])

    for n in range(CHUNKS):
        put_d(n).start()

    def correct(n, weights):
        rising, falling = weights
        for u in range(wide):
            x = n * wide + u
            up = rising * F32(decay ** (u + 1))
            down = falling * F32(decay ** (wide - u))
            for i in range(9):
                held[i, x] = local_ref[i, x] + (up * carry_ref[i] + down * carry_ref[9 + i])
        put_s(n).start()
        return rising * F32(decay**wide), falling * F32(decay**-wide)

    shape = carry_ref.shape[1:]
    ones = jnp.ones(shape, F32)
    lax.fori_loop(0, CHUNKS, correct, (ones, ones * F32(decay ** (cells - wide))))
    for n in range(CHUNKS):
        put_d(n).wait()
        put_s(n).wait()


def shards(velocity):
    comps, cells, layers, span = velocity.shape
    blocks = lax.axis_size("gx")
    ring = blocks // GROUP
    decay, scale = decay_of((cells * blocks / 8.0) ** 2)
    big = (9, cells, layers, span)
    small = (18, layers, span)
    local, deriv, carry = pl.pallas_call(
        functools.partial(exchange_kernel, decay, scale, cells, blocks),
        out_shape=(
            pltpu.VMEM(big, F32),
            pltpu.VMEM(big, F32),
            pltpu.VMEM(small, F32),
        ),
        in_specs=[pl.BlockSpec(memory_space=pl.ANY)],
        out_specs=[pl.BlockSpec(memory_space=pltpu.VMEM)] * 3,
        scratch_shapes=[
            pltpu.VMEM((comps, cells, layers, span), F32),
            pltpu.VMEM((comps, cells, layers, span), F32),
        ]
        + [pltpu.VMEM(small, F32)] * 6
        + [
            pltpu.SemaphoreType.DMA((CHUNKS,)),
            pltpu.SemaphoreType.DMA((CHUNKS, 2)),
            pltpu.SemaphoreType.DMA((CHUNKS, 2)),
            pltpu.SemaphoreType.DMA((3, GROUP)),
            pltpu.SemaphoreType.DMA((3, GROUP)),
            pltpu.SemaphoreType.REGULAR,
            pltpu.SemaphoreType.REGULAR,
            pltpu.SemaphoreType.REGULAR,
        ],
        compiler_params=pltpu.CompilerParams(
            collective_id=0, has_side_effects=True, vmem_limit_bytes=44 << 20
        ),
        name="exchange",
    )(velocity)
    return pl.pallas_call(
        functools.partial(write_kernel, decay, cells),
        out_shape=(jax.ShapeDtypeStruct(big, F32), jax.ShapeDtypeStruct(big, F32)),
        in_specs=[pl.BlockSpec(memory_space=pltpu.VMEM)] * 3,
        out_specs=[pl.BlockSpec(memory_space=pltpu.HBM)] * 2,
        scratch_shapes=[
            pltpu.VMEM(big, F32),
            pltpu.SemaphoreType.DMA((CHUNKS,)),
            pltpu.SemaphoreType.DMA((CHUNKS,)),
        ],
        compiler_params=pltpu.CompilerParams(vmem_limit_bytes=24 << 20),
        name="write",
    )(local, deriv, carry)


def solution(mesh):
    spec = P(None, "gx", "gz", None)
    return jax.shard_map(
        shards, mesh=mesh, in_specs=(spec,), out_specs=(spec, spec), check_vma=False
    )
```

```python
import functools
import math

import jax
import jax.numpy as jnp
from jax import lax
from jax.experimental import pallas as pl
from jax.experimental.pallas import tpu as pltpu
from jax.sharding import PartitionSpec as P

MESH = pl.DeviceIdType.MESH
F32 = jnp.float32
GROUP = 8
CHUNKS = 8
PIECES = 8
HALO = 3
ORDER1 = (0, 7, 1, 6, 2, 5, 3, 4)
ORDER3 = (1, 0, 7, 6, 2, 3, 4, 5)
DERIV = (45.0 / 60.0, -9.0 / 60.0, 1.0 / 60.0)


def decay_of(stiffness):
    half = 0.5 / math.sqrt(stiffness)
    return math.exp(-2.0 * math.asinh(half)), 1.0 / math.sqrt(1.0 + 4.0 * stiffness)


def fields_of(a, b):
    return (
        a[0],
        a[1],
        a[2],
        a[0] * b[0],
        a[0] * b[1],
        a[0] * b[2],
        a[1] * b[1],
        a[1] * b[2],
        a[2] * b[2],
    )


def by_row(index, values):
    out = jnp.full(index.shape, values[0], F32)
    for i, value in enumerate(values[1:], 1):
        out = jnp.where(index == i, F32(value), out)
    return out


def vertical(center, halo, rows):
    total = None
    for k, coef in enumerate(DERIV, 1):
        upper = [
            pltpu.roll(jnp.where(rows >= k, c, h), 8 - k, 0) for c, h in zip(center, halo)
        ]
        lower = [
            pltpu.roll(jnp.where(rows < 8 - k, c, h), k, 0) for c, h in zip(center, halo)
        ]
        above = fields_of([F32(coef) * a for a in upper], upper)
        below = fields_of([F32(coef) * b for b in lower], lower)
        term = [a - b for a, b in zip(above, below)]
        total = term if total is None else [t + s for t, s in zip(total, term)]
    return total


def exchange_kernel(
    decay,
    scale,
    cells,
    blocks,
    v_hbm,
    local_ref,
    deriv_ref,
    carry_ref,
    v_ref,
    halo_ref,
    sums_ref,
    group_ref,
    total_ref,
    ring_ref,
    scan_ref,
    back_ref,
    load_sem,
    halo_send,
    halo_recv,
    send_sem,
    recv_sem,
    group_go,
    y_go,
    z_go,
):
    me = lax.axis_index("gx")
    y = lax.axis_index("gz")
    y_parts = lax.axis_size("gz")
    ring = blocks // GROUP
    z = me // GROUP
    p = lax.rem(me, GROUP)
    above_id = lax.rem(y + 1, y_parts)
    below_id = lax.rem(y + y_parts - 1, y_parts)
    wide = cells // CHUNKS
    rho = decay**cells
    jump = rho**GROUP

    def signal(sem, **device):
        pl.semaphore_signal(sem, inc=1, device_id=device, device_id_type=MESH)

    def in_group(k):
        return lax.rem(p + k, GROUP)

    def group_peer(k):
        return z * GROUP + in_group(k)

    def ring_peer(k):
        return lax.rem(z + k, ring) * GROUP + p

    barrier = pltpu.get_barrier_semaphore()
    even = lax.rem(p, 2) == 0
    for k in range(1, GROUP):

        @pl.when(lax.rem(p + k, 2) == 0)
        def _(k=k):
            signal(barrier, gx=group_peer(k))

    second_chip = p // 2 == 1
    for other in (above_id, below_id):

        @pl.when(second_chip)
        def _(other=other):
            signal(barrier, gx=z * GROUP + 1, gz=other)

        @pl.when(jnp.logical_not(second_chip))
        def _(other=other):
            signal(barrier, gx=me + 1 - lax.rem(p, 2), gz=other)

    def load(n):
        part = pl.ds(n * wide, wide)
        return pltpu.make_async_copy(v_hbm.at[:, part], v_ref.at[:, part], load_sem.at[n])

    for n in range(CHUNKS):
        load(n).start()

    def halo(n, side):
        first, target = ((0, below_id), (8 - HALO, above_id))[side]
        part = pl.ds(n * wide, wide)
        layers = pl.ds(first, HALO)
        return pltpu.make_async_remote_copy(
            src_ref=v_hbm.at[:, part, layers],
            dst_ref=halo_ref.at[:, part, layers],
            send_sem=halo_send,
            recv_sem=halo_recv.at[n],
            device_id={"gz": target},
            device_id_type=MESH,
        )

    def both_halos(part, received):
        layers = pl.ds(0, 2 * HALO)
        return pltpu.make_async_remote_copy(
            src_ref=v_hbm.at[:, part, layers],
            dst_ref=halo_ref.at[:, part, layers],
            send_sem=halo_send,
            recv_sem=received,
            device_id={"gz": above_id},
            device_id_type=MESH,
        )

    shape = v_ref.shape[2:]
    rows = lax.broadcasted_iota(jnp.int32, shape, 0)
    zero = jnp.zeros(shape, F32)

    def velocity(x):
        return [v_ref[c, x] for c in range(3)]

    def scaled_fields(x):
        v = velocity(x)
        return fields_of([F32(scale) * a for a in v], v)

    def forward(n, state):
        load(n).wait()
        ahead, back, weight = state
        for u in range(wide):
            x = n * wide + u
            f = scaled_fields(x)
            ahead = [F32(decay) * a + b for a, b in zip(ahead, f)]
            back = [a + weight * b for a, b in zip(back, f)]
            weight = weight * F32(decay)
            for i in range(9):
                local_ref[i, x] = ahead[i]
        return tuple(ahead), tuple(back), weight

    state = ((zero,) * 9, (zero,) * 9, jnp.ones(shape, F32))
    state = lax.fori_loop(0, CHUNKS, forward, state)
    for i in range(9):
        sums_ref[i] = state[0][i]
        sums_ref[9 + i] = state[1][i]

    def carries(stage, source, target, source_rows, target_rows, peer):
        return pltpu.make_async_remote_copy(
            src_ref=source.at[:, source_rows],
            dst_ref=target.at[:, target_rows],
            send_sem=send_sem.at[stage],
            recv_sem=recv_sem.at[stage],
            device_id={"gx": peer},
            device_id_type=MESH,
        )

    def all_carries(stage, source, target, count):
        every = pl.ds(0, count - 1)
        return carries(stage, source, target, every, every, me)

    def others(own, order, act):
        for to in order:

            @pl.when(own != to)
            def _(to=to):
                act(to)

    def start_group(stage, source, target, order):
        def start(to):
            peer = z * GROUP + to
            carries(stage, source, target, pl.ds(to, 1), pl.ds(p, 1), peer).start()

        others(p, order, start)

    first = all_carries(0, sums_ref, group_ref, GROUP)
    second = all_carries(1, total_ref, ring_ref, ring)
    third = all_carries(2, scan_ref, back_ref, GROUP)

    @pl.when(even)
    def _():
        pl.semaphore_wait(barrier, GROUP - 1)
        signal(group_go, gx=me + 1)

    @pl.when(jnp.logical_not(even))
    def _():
        pl.semaphore_wait(group_go, 1)

    @pl.when(p == 2)
    def _():
        for k in range(1, ring):
            signal(barrier, gx=ring_peer(k) + 1)

    start_group(0, sums_ref, group_ref, ORDER1)

    @pl.when(p == 1)
    def _():
        pl.semaphore_wait(barrier, 8)
        for target in (me - 1, me + 1, me + 2):
            signal(y_go, gx=target)

    @pl.when(jnp.logical_and(jnp.logical_not(even), p >= 5))
    def _():
        pl.semaphore_wait(barrier, 4)
        signal(y_go, gx=me - 1)

    @pl.when(jnp.logical_or(even, p == 3))
    def _():
        pl.semaphore_wait(y_go, 1)

    for n in range(CHUNKS):
        for side in range(2):
            halo(n, side).start()

    def backward(n, behind):
        for u in range(wide):
            x = cells - 1 - (n * wide + u)
            for i in range(9):
                local_ref[i, x] = local_ref[i, x] + behind[i]
            f = scaled_fields(x)
            behind = [F32(decay) * (a + b) for a, b in zip(behind, f)]
        return tuple(behind)

    @pl.when(p == 3)
    def _():
        pl.semaphore_wait(barrier, ring - 1)
        for k in range(1, GROUP):
            signal(z_go, gx=group_peer(k))

    def derive(n, _):
        both_halos(pl.ds(n * wide, wide), halo_recv.at[n]).wait_recv()

        def one(j, _):
            x = n * wide + j
            out = vertical(velocity(x), [halo_ref[c, x] for c in range(3)], rows)
            for i in range(9):
                deriv_ref[i, x] = out[i]
            return 0

        return lax.fori_loop(0, wide, one, 0)

    rising = by_row(rows, [rho**b for b in range(GROUP)])
    sinking = by_row(rows, [rho ** (GROUP - 1 - b) for b in range(GROUP)])
    mine = rows == p
    first.wait_recv()
    for i in range(18):
        held = jnp.where(mine, sums_ref[i], group_ref[i])
        group_ref[i] = held
        part = held * (sinking if i < 9 else rising)
        total_ref[i] = jnp.broadcast_to(jnp.sum(part, axis=0, keepdims=True), shape)

    @pl.when(p != 3)
    def _():
        pl.semaphore_wait(z_go, 1)

    def start_ring(*planes):
        def start(to):
            peer = to * GROUP + p
            carries(1, total_ref, ring_ref, pl.ds(z, 1), pl.ds(z, 1), peer).start()

        others(z, planes, start)

    start_ring(0)
    for i in range(18):
        if i < 9:
            run = jnp.where(rows >= 1, pltpu.roll(group_ref[i], 1, 0), F32(0))
            for s in (1, 2, 4):
                moved = jnp.where(rows >= s, pltpu.roll(run, s, 0), F32(0))
                run = run + F32(rho**s) * moved
        else:
            run = jnp.where(rows < 7, pltpu.roll(group_ref[i], 7, 0), F32(0))
            for s in (1, 2, 4):
                moved = jnp.where(rows < 8 - s, pltpu.roll(run, 8 - s, 0), F32(0))
                run = run + F32(rho**s) * moved
        scan_ref[i] = run

    start_ring(1)
    half = CHUNKS // 2
    behind = lax.fori_loop(0, half, backward, (zero,) * 9)
    start_ring(2, 3)
    lax.fori_loop(half, CHUNKS, backward, behind)
    start_ring(*range(4, ring))

    closed = 1.0 / (1.0 - jump**ring)
    powers = [closed * jump**e for e in range(ring)]
    ahead_weight = by_row(lax.rem(z - rows + 2 * ring - 1, ring), powers)
    back_weight = by_row(lax.rem(rows - z + 2 * ring - 1, ring), powers)
    own = rows == z
    second.wait_recv()
    for i in range(18):
        held = jnp.where(own, total_ref[i], ring_ref[i])
        part = held * (ahead_weight if i < 9 else back_weight)
        entering = jnp.broadcast_to(jnp.sum(part, axis=0, keepdims=True), shape)
        scan_ref[i] = scan_ref[i] + (rising if i < 9 else sinking) * entering

    start_group(2, scan_ref, back_ref, ORDER3)

    lax.fori_loop(0, CHUNKS, derive, 0)

    third.wait_recv()
    for i in range(18):
        carry_ref[i] = jnp.where(mine, scan_ref[i], back_ref[i])

    for copy in (first, second, third):
        copy.wait_send()
    both_halos(pl.ds(0, cells), halo_recv.at[0]).wait_send()


def write_kernel(decay, cells, local_ref, deriv_ref, carry_ref, out_s, out_d, held, sem_s, sem_d):
    wide = cells // PIECES

    def put_d(n):
        part = pl.ds(n * wide, wide)
        return pltpu.make_async_copy(deriv_ref.at[:, part], out_d.at[:, part], sem_d)

    def put_s(n):
        part = pl.ds(n * wide, wide)
        return pltpu.make_async_copy(held.at[:, part], out_s.at[:, part], sem_s)

    for n in range(PIECES):
        put_d(n).start()

    def correct(n, weights):
        rising, falling = weights
        for u in range(wide):
            x = n * wide + u
            up = rising * F32(decay ** (u + 1))
            down = falling * F32(decay ** (wide - u))
            for i in range(9):
                held[i, x] = local_ref[i, x] + (up * carry_ref[i] + down * carry_ref[9 + i])
        put_s(n).start()
        return rising * F32(decay**wide), falling * F32(decay**-wide)

    shape = carry_ref.shape[1:]
    ones = jnp.ones(shape, F32)
    lax.fori_loop(0, PIECES, correct, (ones, ones * F32(decay ** (cells - wide))))
    pltpu.make_async_copy(deriv_ref, out_d, sem_d).wait()
    pltpu.make_async_copy(held, out_s, sem_s).wait()


def shards(velocity):
    comps, cells, layers, span = velocity.shape
    blocks = lax.axis_size("gx")
    ring = blocks // GROUP
    decay, scale = decay_of((cells * blocks / 8.0) ** 2)
    big = (9, cells, layers, span)
    small = (18, layers, span)
    local, deriv, carry = pl.pallas_call(
        functools.partial(exchange_kernel, decay, scale, cells, blocks),
        out_shape=(
            pltpu.VMEM(big, F32),
            pltpu.VMEM(big, F32),
            pltpu.VMEM(small, F32),
        ),
        in_specs=[pl.BlockSpec(memory_space=pl.ANY)],
        out_specs=[pl.BlockSpec(memory_space=pltpu.VMEM)] * 3,
        scratch_shapes=[
            pltpu.VMEM((comps, cells, layers, span), F32),
            pltpu.VMEM((comps, cells, layers, span), F32),
        ]
        + [pltpu.VMEM(small, F32)] * 6
        + [
            pltpu.SemaphoreType.DMA((CHUNKS,)),
            pltpu.SemaphoreType.DMA,
            pltpu.SemaphoreType.DMA((CHUNKS,)),
            pltpu.SemaphoreType.DMA((3,)),
            pltpu.SemaphoreType.DMA((3,)),
            pltpu.SemaphoreType.REGULAR,
            pltpu.SemaphoreType.REGULAR,
            pltpu.SemaphoreType.REGULAR,
        ],
        compiler_params=pltpu.CompilerParams(
            collective_id=0, has_side_effects=True, vmem_limit_bytes=44 << 20
        ),
        name="exchange",
    )(velocity)
    return pl.pallas_call(
        functools.partial(write_kernel, decay, cells),
        out_shape=(jax.ShapeDtypeStruct(big, F32), jax.ShapeDtypeStruct(big, F32)),
        in_specs=[pl.BlockSpec(memory_space=pltpu.VMEM)] * 3,
        out_specs=[pl.BlockSpec(memory_space=pltpu.HBM)] * 2,
        scratch_shapes=[
            pltpu.VMEM(big, F32),
            pltpu.SemaphoreType.DMA,
            pltpu.SemaphoreType.DMA,
        ],
        compiler_params=pltpu.CompilerParams(vmem_limit_bytes=24 << 20),
        name="write",
    )(local, deriv, carry)


def solution(mesh):
    spec = P(None, "gx", "gz", None)
    return jax.shard_map(
        shards, mesh=mesh, in_specs=(spec,), out_specs=(spec, spec), check_vma=False
    )
```

```python
import functools
import math

import jax
import jax.numpy as jnp
from jax import lax
from jax.experimental import pallas as pl
from jax.experimental.pallas import tpu as pltpu
from jax.sharding import PartitionSpec as P

MESH = pl.DeviceIdType.MESH
F32 = jnp.float32
GROUP = 8
CHUNKS = 8
PIECES = 8
PARTS = (32, 16, 8, 8)
HALO = 3
ORDER1 = (0, 7, 1, 6, 2, 5, 3, 4)
ORDER3 = (1, 0, 7, 6, 2, 3, 4, 5)
DERIV = (45.0 / 60.0, -9.0 / 60.0, 1.0 / 60.0)


def decay_of(stiffness):
    half = 0.5 / math.sqrt(stiffness)
    return math.exp(-2.0 * math.asinh(half)), 1.0 / math.sqrt(1.0 + 4.0 * stiffness)


def fields_of(a, b):
    return (
        a[0],
        a[1],
        a[2],
        a[0] * b[0],
        a[0] * b[1],
        a[0] * b[2],
        a[1] * b[1],
        a[1] * b[2],
        a[2] * b[2],
    )


def by_row(index, values):
    out = jnp.full(index.shape, values[0], F32)
    for i, value in enumerate(values[1:], 1):
        out = jnp.where(index == i, F32(value), out)
    return out


def vertical(center, halo, rows):
    total = None
    for k, coef in enumerate(DERIV, 1):
        upper = [
            pltpu.roll(jnp.where(rows >= k, c, h), 8 - k, 0) for c, h in zip(center, halo)
        ]
        lower = [
            pltpu.roll(jnp.where(rows < 8 - k, c, h), k, 0) for c, h in zip(center, halo)
        ]
        above = fields_of([F32(coef) * a for a in upper], upper)
        below = fields_of([F32(coef) * b for b in lower], lower)
        term = [a - b for a, b in zip(above, below)]
        total = term if total is None else [t + s for t, s in zip(total, term)]
    return total


def exchange_kernel(
    decay,
    scale,
    cells,
    blocks,
    v_hbm,
    local_ref,
    deriv_ref,
    carry_ref,
    v_ref,
    halo_ref,
    sums_ref,
    group_ref,
    total_ref,
    ring_ref,
    scan_ref,
    back_ref,
    load_sem,
    halo_send,
    halo_recv,
    send_sem,
    recv_sem,
    group_go,
    y_go,
    z_go,
):
    me = lax.axis_index("gx")
    y = lax.axis_index("gz")
    y_parts = lax.axis_size("gz")
    ring = blocks // GROUP
    z = me // GROUP
    p = lax.rem(me, GROUP)
    above_id = lax.rem(y + 1, y_parts)
    below_id = lax.rem(y + y_parts - 1, y_parts)
    wide = cells // CHUNKS
    rho = decay**cells
    jump = rho**GROUP

    def signal(sem, **device):
        pl.semaphore_signal(sem, inc=1, device_id=device, device_id_type=MESH)

    def in_group(k):
        return lax.rem(p + k, GROUP)

    def group_peer(k):
        return z * GROUP + in_group(k)

    def ring_peer(k):
        return lax.rem(z + k, ring) * GROUP + p

    barrier = pltpu.get_barrier_semaphore()
    even = lax.rem(p, 2) == 0
    for k in range(1, GROUP):

        @pl.when(lax.rem(p + k, 2) == 0)
        def _(k=k):
            signal(barrier, gx=group_peer(k))

    second_chip = p // 2 == 1
    for other in (above_id, below_id):

        @pl.when(second_chip)
        def _(other=other):
            signal(barrier, gx=z * GROUP + 1, gz=other)

        @pl.when(jnp.logical_not(second_chip))
        def _(other=other):
            signal(barrier, gx=me + 1 - lax.rem(p, 2), gz=other)

    def load(n):
        part = pl.ds(n * wide, wide)
        return pltpu.make_async_copy(v_hbm.at[:, part], v_ref.at[:, part], load_sem.at[n])

    for n in range(CHUNKS):
        load(n).start()

    def halo(n, side):
        first, target = ((0, below_id), (8 - HALO, above_id))[side]
        part = pl.ds(sum(PARTS[:n]), PARTS[n])
        layers = pl.ds(first, HALO)
        return pltpu.make_async_remote_copy(
            src_ref=v_hbm.at[:, part, layers],
            dst_ref=halo_ref.at[:, part, layers],
            send_sem=halo_send,
            recv_sem=halo_recv.at[n],
            device_id={"gz": target},
            device_id_type=MESH,
        )

    def both_halos(part, received):
        layers = pl.ds(0, 2 * HALO)
        return pltpu.make_async_remote_copy(
            src_ref=v_hbm.at[:, part, layers],
            dst_ref=halo_ref.at[:, part, layers],
            send_sem=halo_send,
            recv_sem=received,
            device_id={"gz": above_id},
            device_id_type=MESH,
        )

    shape = v_ref.shape[2:]
    rows = lax.broadcasted_iota(jnp.int32, shape, 0)
    zero = jnp.zeros(shape, F32)

    def velocity(x):
        return [v_ref[c, x] for c in range(3)]

    def scaled_fields(x):
        v = velocity(x)
        return fields_of([F32(scale) * a for a in v], v)

    def forward(n, state):
        load(n).wait()
        ahead, back, weight = state
        for u in range(wide):
            x = n * wide + u
            f = scaled_fields(x)
            ahead = [F32(decay) * a + b for a, b in zip(ahead, f)]
            back = [a + weight * b for a, b in zip(back, f)]
            weight = weight * F32(decay)
            for i in range(9):
                local_ref[i, x] = ahead[i]
        return tuple(ahead), tuple(back), weight

    def pass_on():
        pl.semaphore_wait(barrier, GROUP - 1)
        signal(group_go, gx=me + 1)

    pl.when(jnp.logical_and(even, p >= GROUP // 2))(pass_on)

    state = ((zero,) * 9, (zero,) * 9, jnp.ones(shape, F32))
    state = lax.fori_loop(0, CHUNKS, forward, state)
    for i in range(9):
        sums_ref[i] = state[0][i]
        sums_ref[9 + i] = state[1][i]

    def carries(stage, source, target, source_rows, target_rows, peer):
        return pltpu.make_async_remote_copy(
            src_ref=source.at[:, source_rows],
            dst_ref=target.at[:, target_rows],
            send_sem=send_sem.at[stage],
            recv_sem=recv_sem.at[stage],
            device_id={"gx": peer},
            device_id_type=MESH,
        )

    def all_carries(stage, source, target, count):
        every = pl.ds(0, count - 1)
        return carries(stage, source, target, every, every, me)

    def others(own, order, act):
        for to in order:

            @pl.when(own != to)
            def _(to=to):
                act(to)

    def start_group(stage, source, target, order):
        def start(to):
            peer = z * GROUP + to
            carries(stage, source, target, pl.ds(to, 1), pl.ds(p, 1), peer).start()

        others(p, order, start)

    first = all_carries(0, sums_ref, group_ref, GROUP)
    second = all_carries(1, total_ref, ring_ref, ring)
    third = all_carries(2, scan_ref, back_ref, GROUP)

    pl.when(jnp.logical_and(even, p < GROUP // 2))(pass_on)

    @pl.when(jnp.logical_not(even))
    def _():
        pl.semaphore_wait(group_go, 1)

    @pl.when(p == 2)
    def _():
        for k in range(1, ring):
            signal(barrier, gx=ring_peer(k) + 1)

    start_group(0, sums_ref, group_ref, ORDER1)

    @pl.when(p == 1)
    def _():
        pl.semaphore_wait(barrier, 8)
        for target in (me - 1, me + 1, me + 2):
            signal(y_go, gx=target)

    @pl.when(jnp.logical_and(jnp.logical_not(even), p >= 5))
    def _():
        pl.semaphore_wait(barrier, 4)
        signal(y_go, gx=me - 1)

    @pl.when(jnp.logical_or(even, p == 3))
    def _():
        pl.semaphore_wait(y_go, 1)

    for n in range(len(PARTS)):
        for side in range(2):
            halo(n, side).start()

    def backward(n, behind):
        for u in range(wide):
            x = cells - 1 - (n * wide + u)
            for i in range(9):
                local_ref[i, x] = local_ref[i, x] + behind[i]
            f = scaled_fields(x)
            behind = [F32(decay) * (a + b) for a, b in zip(behind, f)]
        return tuple(behind)

    @pl.when(p == 3)
    def _():
        pl.semaphore_wait(barrier, ring - 1)
        for k in range(1, GROUP):
            signal(z_go, gx=group_peer(k))

    def derive(n):
        start = sum(PARTS[:n])
        both_halos(pl.ds(start, PARTS[n]), halo_recv.at[n]).wait_recv()

        def one(j, _):
            x = start + j
            out = vertical(velocity(x), [halo_ref[c, x] for c in range(3)], rows)
            for i in range(9):
                deriv_ref[i, x] = out[i]
            return 0

        lax.fori_loop(0, PARTS[n], one, 0)

    rising = by_row(rows, [rho**b for b in range(GROUP)])
    sinking = by_row(rows, [rho ** (GROUP - 1 - b) for b in range(GROUP)])
    mine = rows == p
    first.wait_recv()
    for i in range(18):
        held = jnp.where(mine, sums_ref[i], group_ref[i])
        group_ref[i] = held
        part = held * (sinking if i < 9 else rising)
        total_ref[i] = jnp.broadcast_to(jnp.sum(part, axis=0, keepdims=True), shape)

    @pl.when(p != 3)
    def _():
        pl.semaphore_wait(z_go, 1)

    def start_ring(*planes):
        def start(to):
            peer = to * GROUP + p
            carries(1, total_ref, ring_ref, pl.ds(z, 1), pl.ds(z, 1), peer).start()

        others(z, planes, start)

    start_ring(0)
    for i in range(18):
        if i < 9:
            run = jnp.where(rows >= 1, pltpu.roll(group_ref[i], 1, 0), F32(0))
            for s in (1, 2, 4):
                moved = jnp.where(rows >= s, pltpu.roll(run, s, 0), F32(0))
                run = run + F32(rho**s) * moved
        else:
            run = jnp.where(rows < 7, pltpu.roll(group_ref[i], 7, 0), F32(0))
            for s in (1, 2, 4):
                moved = jnp.where(rows < 8 - s, pltpu.roll(run, 8 - s, 0), F32(0))
                run = run + F32(rho**s) * moved
        scan_ref[i] = run

    start_ring(1)
    half = CHUNKS // 2
    behind = lax.fori_loop(0, half, backward, (zero,) * 9)
    start_ring(2, 3)
    lax.fori_loop(half, CHUNKS, backward, behind)
    start_ring(*range(4, ring))

    closed = 1.0 / (1.0 - jump**ring)
    powers = [closed * jump**e for e in range(ring)]
    ahead_weight = by_row(lax.rem(z - rows + 2 * ring - 1, ring), powers)
    back_weight = by_row(lax.rem(rows - z + 2 * ring - 1, ring), powers)
    own = rows == z
    second.wait_recv()
    for i in range(18):
        held = jnp.where(own, total_ref[i], ring_ref[i])
        part = held * (ahead_weight if i < 9 else back_weight)
        entering = jnp.broadcast_to(jnp.sum(part, axis=0, keepdims=True), shape)
        scan_ref[i] = scan_ref[i] + (rising if i < 9 else sinking) * entering

    start_group(2, scan_ref, back_ref, ORDER3)

    for n in range(len(PARTS)):
        derive(n)

    third.wait_recv()
    for i in range(18):
        carry_ref[i] = jnp.where(mine, scan_ref[i], back_ref[i])

    for copy in (first, second, third):
        copy.wait_send()
    both_halos(pl.ds(0, cells), halo_recv.at[0]).wait_send()


def write_kernel(decay, cells, local_ref, deriv_ref, carry_ref, out_s, out_d, held, sem_s, sem_d):
    wide = cells // PIECES

    def put_d(n):
        part = pl.ds(n * wide, wide)
        return pltpu.make_async_copy(deriv_ref.at[:, part], out_d.at[:, part], sem_d)

    def put_s(n):
        part = pl.ds(n * wide, wide)
        return pltpu.make_async_copy(held.at[:, part], out_s.at[:, part], sem_s)

    for n in range(PIECES):
        put_d(n).start()

    def correct(n, weights):
        rising, falling = weights
        for u in range(wide):
            x = n * wide + u
            up = rising * F32(decay ** (u + 1))
            down = falling * F32(decay ** (wide - u))
            for i in range(9):
                held[i, x] = local_ref[i, x] + (up * carry_ref[i] + down * carry_ref[9 + i])
        put_s(n).start()
        return rising * F32(decay**wide), falling * F32(decay**-wide)

    shape = carry_ref.shape[1:]
    ones = jnp.ones(shape, F32)
    lax.fori_loop(0, PIECES, correct, (ones, ones * F32(decay ** (cells - wide))))
    pltpu.make_async_copy(deriv_ref, out_d, sem_d).wait()
    pltpu.make_async_copy(held, out_s, sem_s).wait()


def shards(velocity):
    comps, cells, layers, span = velocity.shape
    blocks = lax.axis_size("gx")
    ring = blocks // GROUP
    decay, scale = decay_of((cells * blocks / 8.0) ** 2)
    big = (9, cells, layers, span)
    small = (18, layers, span)
    local, deriv, carry = pl.pallas_call(
        functools.partial(exchange_kernel, decay, scale, cells, blocks),
        out_shape=(
            pltpu.VMEM(big, F32),
            pltpu.VMEM(big, F32),
            pltpu.VMEM(small, F32),
        ),
        in_specs=[pl.BlockSpec(memory_space=pl.ANY)],
        out_specs=[pl.BlockSpec(memory_space=pltpu.VMEM)] * 3,
        scratch_shapes=[
            pltpu.VMEM((comps, cells, layers, span), F32),
            pltpu.VMEM((comps, cells, layers, span), F32),
        ]
        + [pltpu.VMEM(small, F32)] * 6
        + [
            pltpu.SemaphoreType.DMA((CHUNKS,)),
            pltpu.SemaphoreType.DMA,
            pltpu.SemaphoreType.DMA((len(PARTS),)),
            pltpu.SemaphoreType.DMA((3,)),
            pltpu.SemaphoreType.DMA((3,)),
            pltpu.SemaphoreType.REGULAR,
            pltpu.SemaphoreType.REGULAR,
            pltpu.SemaphoreType.REGULAR,
        ],
        compiler_params=pltpu.CompilerParams(
            collective_id=0, has_side_effects=True, vmem_limit_bytes=44 << 20
        ),
        name="exchange",
    )(velocity)
    return pl.pallas_call(
        functools.partial(write_kernel, decay, cells),
        out_shape=(jax.ShapeDtypeStruct(big, F32), jax.ShapeDtypeStruct(big, F32)),
        in_specs=[pl.BlockSpec(memory_space=pltpu.VMEM)] * 3,
        out_specs=[pl.BlockSpec(memory_space=pltpu.HBM)] * 2,
        scratch_shapes=[
            pltpu.VMEM(big, F32),
            pltpu.SemaphoreType.DMA,
            pltpu.SemaphoreType.DMA,
        ],
        compiler_params=pltpu.CompilerParams(vmem_limit_bytes=24 << 20),
        name="write",
    )(local, deriv, carry)


def solution(mesh):
    spec = P(None, "gx", "gz", None)
    return jax.shard_map(
        shards, mesh=mesh, in_specs=(spec,), out_specs=(spec, spec), check_vma=False
    )
```

```python
import functools
import math

import jax
import jax.numpy as jnp
from jax import lax
from jax.experimental import pallas as pl
from jax.experimental.pallas import tpu as pltpu
from jax.sharding import PartitionSpec as P

MESH = pl.DeviceIdType.MESH
F32 = jnp.float32
GROUP = 8
CHUNKS = 8
PIECES = 8
PARTS = (32, 16, 8, 8)
HALO = 3
ORDER1 = (6, 0, 4, 2, 7, 1, 5, 3)
ORDER3 = (1, 0, 7, 6, 2, 3, 4, 5)
DERIV = (45.0 / 60.0, -9.0 / 60.0, 1.0 / 60.0)


def decay_of(stiffness):
    half = 0.5 / math.sqrt(stiffness)
    return math.exp(-2.0 * math.asinh(half)), 1.0 / math.sqrt(1.0 + 4.0 * stiffness)


def fields_of(a, b):
    return (
        a[0],
        a[1],
        a[2],
        a[0] * b[0],
        a[0] * b[1],
        a[0] * b[2],
        a[1] * b[1],
        a[1] * b[2],
        a[2] * b[2],
    )


def by_row(index, values):
    out = jnp.full(index.shape, values[0], F32)
    for i, value in enumerate(values[1:], 1):
        out = jnp.where(index == i, F32(value), out)
    return out


def vertical(center, halo, rows):
    total = None
    for k, coef in enumerate(DERIV, 1):
        upper = [
            pltpu.roll(jnp.where(rows >= k, c, h), 8 - k, 0) for c, h in zip(center, halo)
        ]
        lower = [
            pltpu.roll(jnp.where(rows < 8 - k, c, h), k, 0) for c, h in zip(center, halo)
        ]
        above = fields_of([F32(coef) * a for a in upper], upper)
        below = fields_of([F32(coef) * b for b in lower], lower)
        term = [a - b for a, b in zip(above, below)]
        total = term if total is None else [t + s for t, s in zip(total, term)]
    return total


def exchange_kernel(
    decay,
    scale,
    cells,
    blocks,
    v_hbm,
    local_ref,
    deriv_ref,
    carry_ref,
    v_ref,
    halo_ref,
    sums_ref,
    group_ref,
    total_ref,
    ring_ref,
    scan_ref,
    back_ref,
    load_sem,
    halo_send,
    halo_recv,
    send_sem,
    recv_sem,
    group_go,
    y_go,
    z_go,
):
    me = lax.axis_index("gx")
    y = lax.axis_index("gz")
    y_parts = lax.axis_size("gz")
    ring = blocks // GROUP
    z = me // GROUP
    p = lax.rem(me, GROUP)
    above_id = lax.rem(y + 1, y_parts)
    below_id = lax.rem(y + y_parts - 1, y_parts)
    wide = cells // CHUNKS
    rho = decay**cells
    jump = rho**GROUP

    def signal(sem, **device):
        pl.semaphore_signal(sem, inc=1, device_id=device, device_id_type=MESH)

    def in_group(k):
        return lax.rem(p + k, GROUP)

    def group_peer(k):
        return z * GROUP + in_group(k)

    def ring_peer(k):
        return lax.rem(z + k, ring) * GROUP + p

    barrier = pltpu.get_barrier_semaphore()
    even = lax.rem(p, 2) == 0
    for k in range(1, GROUP):

        @pl.when(lax.rem(p + k, 2) == 0)
        def _(k=k):
            signal(barrier, gx=group_peer(k))

    third_chip = p // 2 == 2
    for other in (above_id, below_id):

        @pl.when(third_chip)
        def _(other=other):
            signal(barrier, gx=z * GROUP + 7, gz=other)

        @pl.when(jnp.logical_not(third_chip))
        def _(other=other):
            signal(barrier, gx=me + 1 - lax.rem(p, 2), gz=other)

    def load(n):
        part = pl.ds(n * wide, wide)
        return pltpu.make_async_copy(v_hbm.at[:, part], v_ref.at[:, part], load_sem.at[n])

    for n in range(CHUNKS):
        load(n).start()

    def halo(n, side):
        first, target = ((0, below_id), (8 - HALO, above_id))[side]
        part = pl.ds(sum(PARTS[:n]), PARTS[n])
        layers = pl.ds(first, HALO)
        return pltpu.make_async_remote_copy(
            src_ref=v_hbm.at[:, part, layers],
            dst_ref=halo_ref.at[:, part, layers],
            send_sem=halo_send,
            recv_sem=halo_recv.at[n],
            device_id={"gz": target},
            device_id_type=MESH,
        )

    def both_halos(part, received):
        layers = pl.ds(0, 2 * HALO)
        return pltpu.make_async_remote_copy(
            src_ref=v_hbm.at[:, part, layers],
            dst_ref=halo_ref.at[:, part, layers],
            send_sem=halo_send,
            recv_sem=received,
            device_id={"gz": above_id},
            device_id_type=MESH,
        )

    shape = v_ref.shape[2:]
    rows = lax.broadcasted_iota(jnp.int32, shape, 0)
    zero = jnp.zeros(shape, F32)

    def velocity(x):
        return [v_ref[c, x] for c in range(3)]

    def scaled_fields(x):
        v = velocity(x)
        return fields_of([F32(scale) * a for a in v], v)

    def forward(n, state):
        load(n).wait()
        ahead, back, weight = state
        for u in range(wide):
            x = n * wide + u
            f = scaled_fields(x)
            ahead = [F32(decay) * a + b for a, b in zip(ahead, f)]
            back = [a + weight * b for a, b in zip(back, f)]
            weight = weight * F32(decay)
            for i in range(9):
                local_ref[i, x] = ahead[i]
        return tuple(ahead), tuple(back), weight

    def pass_on():
        pl.semaphore_wait(barrier, GROUP - 1)
        signal(group_go, gx=me + 1)

    pl.when(jnp.logical_and(even, p >= GROUP // 2))(pass_on)

    state = ((zero,) * 9, (zero,) * 9, jnp.ones(shape, F32))
    state = lax.fori_loop(0, CHUNKS, forward, state)
    for i in range(9):
        sums_ref[i] = state[0][i]
        sums_ref[9 + i] = state[1][i]

    def carries(stage, source, target, source_rows, target_rows, peer):
        return pltpu.make_async_remote_copy(
            src_ref=source.at[:, source_rows],
            dst_ref=target.at[:, target_rows],
            send_sem=send_sem.at[stage],
            recv_sem=recv_sem.at[stage],
            device_id={"gx": peer},
            device_id_type=MESH,
        )

    def all_carries(stage, source, target, count):
        every = pl.ds(0, count - 1)
        return carries(stage, source, target, every, every, me)

    def others(own, order, act):
        for to in order:

            @pl.when(own != to)
            def _(to=to):
                act(to)

    def start_group(stage, source, target, order):
        def start(to):
            peer = z * GROUP + to
            carries(stage, source, target, pl.ds(to, 1), pl.ds(p, 1), peer).start()

        others(p, order, start)

    first = all_carries(0, sums_ref, group_ref, GROUP)
    second = all_carries(1, total_ref, ring_ref, ring)
    third = all_carries(2, scan_ref, back_ref, GROUP)

    pl.when(jnp.logical_and(even, p < GROUP // 2))(pass_on)

    @pl.when(jnp.logical_not(even))
    def _():
        pl.semaphore_wait(group_go, 1)

    @pl.when(p == 4)
    def _():
        for k in range(1, ring):
            signal(barrier, gx=ring_peer(k) + 1)

    start_group(0, sums_ref, group_ref, ORDER1)

    @pl.when(p == 7)
    def _():
        pl.semaphore_wait(barrier, 8)
        for target in (me - 1, me - 2, me - 3):
            signal(y_go, gx=target)

    @pl.when(jnp.logical_and(jnp.logical_not(even), p < 5))
    def _():
        pl.semaphore_wait(barrier, 4)
        signal(y_go, gx=me - 1)

    @pl.when(jnp.logical_or(even, p == 5))
    def _():
        pl.semaphore_wait(y_go, 1)

    for n in range(len(PARTS)):
        for side in range(2):
            halo(n, side).start()

    def backward(n, behind):
        for u in range(wide):
            x = cells - 1 - (n * wide + u)
            for i in range(9):
                local_ref[i, x] = local_ref[i, x] + behind[i]
            f = scaled_fields(x)
            behind = [F32(decay) * (a + b) for a, b in zip(behind, f)]
        return tuple(behind)

    @pl.when(p == 5)
    def _():
        pl.semaphore_wait(barrier, ring - 1)
        for k in range(1, GROUP):
            signal(z_go, gx=group_peer(k))

    def derive(n):
        start = sum(PARTS[:n])
        both_halos(pl.ds(start, PARTS[n]), halo_recv.at[n]).wait_recv()

        def one(j, _):
            x = start + j
            out = vertical(velocity(x), [halo_ref[c, x] for c in range(3)], rows)
            for i in range(9):
                deriv_ref[i, x] = out[i]
            return 0

        lax.fori_loop(0, PARTS[n], one, 0)

    rising = by_row(rows, [rho**b for b in range(GROUP)])
    sinking = by_row(rows, [rho ** (GROUP - 1 - b) for b in range(GROUP)])
    mine = rows == p
    first.wait_recv()
    for i in range(18):
        held = jnp.where(mine, sums_ref[i], group_ref[i])
        group_ref[i] = held
        part = held * (sinking if i < 9 else rising)
        total_ref[i] = jnp.broadcast_to(jnp.sum(part, axis=0, keepdims=True), shape)

    @pl.when(p != 5)
    def _():
        pl.semaphore_wait(z_go, 1)

    def start_ring(*planes):
        def start(to):
            peer = to * GROUP + p
            carries(1, total_ref, ring_ref, pl.ds(z, 1), pl.ds(z, 1), peer).start()

        others(z, planes, start)

    start_ring(0)
    for i in range(18):
        if i < 9:
            run = jnp.where(rows >= 1, pltpu.roll(group_ref[i], 1, 0), F32(0))
            for s in (1, 2, 4):
                moved = jnp.where(rows >= s, pltpu.roll(run, s, 0), F32(0))
                run = run + F32(rho**s) * moved
        else:
            run = jnp.where(rows < 7, pltpu.roll(group_ref[i], 7, 0), F32(0))
            for s in (1, 2, 4):
                moved = jnp.where(rows < 8 - s, pltpu.roll(run, 8 - s, 0), F32(0))
                run = run + F32(rho**s) * moved
        scan_ref[i] = run

    start_ring(1)
    half = CHUNKS // 2
    behind = lax.fori_loop(0, half, backward, (zero,) * 9)
    start_ring(2, 3)
    lax.fori_loop(half, CHUNKS, backward, behind)
    start_ring(*range(4, ring))

    closed = 1.0 / (1.0 - jump**ring)
    powers = [closed * jump**e for e in range(ring)]
    ahead_weight = by_row(lax.rem(z - rows + 2 * ring - 1, ring), powers)
    back_weight = by_row(lax.rem(rows - z + 2 * ring - 1, ring), powers)
    own = rows == z
    second.wait_recv()
    for i in range(18):
        held = jnp.where(own, total_ref[i], ring_ref[i])
        part = held * (ahead_weight if i < 9 else back_weight)
        entering = jnp.broadcast_to(jnp.sum(part, axis=0, keepdims=True), shape)
        scan_ref[i] = scan_ref[i] + (rising if i < 9 else sinking) * entering

    start_group(2, scan_ref, back_ref, ORDER3)

    for n in range(len(PARTS)):
        derive(n)

    third.wait_recv()
    for i in range(18):
        carry_ref[i] = jnp.where(mine, scan_ref[i], back_ref[i])

    for copy in (first, second, third):
        copy.wait_send()
    both_halos(pl.ds(0, cells), halo_recv.at[0]).wait_send()


def write_kernel(decay, cells, local_ref, deriv_ref, carry_ref, out_s, out_d, held, sem_s, sem_d):
    wide = cells // PIECES

    def put_d(n):
        part = pl.ds(n * wide, wide)
        return pltpu.make_async_copy(deriv_ref.at[:, part], out_d.at[:, part], sem_d)

    def put_s(n):
        part = pl.ds(n * wide, wide)
        return pltpu.make_async_copy(held.at[:, part], out_s.at[:, part], sem_s)

    for n in range(PIECES):
        put_d(n).start()

    def correct(n, weights):
        rising, falling = weights
        for u in range(wide):
            x = n * wide + u
            up = rising * F32(decay ** (u + 1))
            down = falling * F32(decay ** (wide - u))
            for i in range(9):
                held[i, x] = local_ref[i, x] + (up * carry_ref[i] + down * carry_ref[9 + i])
        put_s(n).start()
        return rising * F32(decay**wide), falling * F32(decay**-wide)

    shape = carry_ref.shape[1:]
    ones = jnp.ones(shape, F32)
    lax.fori_loop(0, PIECES, correct, (ones, ones * F32(decay ** (cells - wide))))
    pltpu.make_async_copy(deriv_ref, out_d, sem_d).wait()
    pltpu.make_async_copy(held, out_s, sem_s).wait()


def shards(velocity):
    comps, cells, layers, span = velocity.shape
    blocks = lax.axis_size("gx")
    ring = blocks // GROUP
    decay, scale = decay_of((cells * blocks / 8.0) ** 2)
    big = (9, cells, layers, span)
    small = (18, layers, span)
    local, deriv, carry = pl.pallas_call(
        functools.partial(exchange_kernel, decay, scale, cells, blocks),
        out_shape=(
            pltpu.VMEM(big, F32),
            pltpu.VMEM(big, F32),
            pltpu.VMEM(small, F32),
        ),
        in_specs=[pl.BlockSpec(memory_space=pl.ANY)],
        out_specs=[pl.BlockSpec(memory_space=pltpu.VMEM)] * 3,
        scratch_shapes=[
            pltpu.VMEM((comps, cells, layers, span), F32),
            pltpu.VMEM((comps, cells, layers, span), F32),
        ]
        + [pltpu.VMEM(small, F32)] * 6
        + [
            pltpu.SemaphoreType.DMA((CHUNKS,)),
            pltpu.SemaphoreType.DMA,
            pltpu.SemaphoreType.DMA((len(PARTS),)),
            pltpu.SemaphoreType.DMA((3,)),
            pltpu.SemaphoreType.DMA((3,)),
            pltpu.SemaphoreType.REGULAR,
            pltpu.SemaphoreType.REGULAR,
            pltpu.SemaphoreType.REGULAR,
        ],
        compiler_params=pltpu.CompilerParams(
            collective_id=0, has_side_effects=True, vmem_limit_bytes=44 << 20
        ),
        name="exchange",
    )(velocity)
    return pl.pallas_call(
        functools.partial(write_kernel, decay, cells),
        out_shape=(jax.ShapeDtypeStruct(big, F32), jax.ShapeDtypeStruct(big, F32)),
        in_specs=[pl.BlockSpec(memory_space=pltpu.VMEM)] * 3,
        out_specs=[pl.BlockSpec(memory_space=pltpu.HBM)] * 2,
        scratch_shapes=[
            pltpu.VMEM(big, F32),
            pltpu.SemaphoreType.DMA,
            pltpu.SemaphoreType.DMA,
        ],
        compiler_params=pltpu.CompilerParams(vmem_limit_bytes=24 << 20),
        name="write",
    )(local, deriv, carry)


def solution(mesh):
    spec = P(None, "gx", "gz", None)
    return jax.shard_map(
        shards, mesh=mesh, in_specs=(spec,), out_specs=(spec, spec), check_vma=False
    )
```

```python
import functools
import math

import jax
import jax.numpy as jnp
from jax import lax
from jax.experimental import pallas as pl
from jax.experimental.pallas import tpu as pltpu
from jax.sharding import PartitionSpec as P

MESH = pl.DeviceIdType.MESH
F32 = jnp.float32
GROUP = 8
CHUNKS = 8
PIECES = 8
LOADS = 2
PARTS = (40, 16, 8)
HALO = 3
ORDER1 = (6, 0, 4, 2, 7, 1, 5, 3)
ORDER3 = (1, 0, 7, 6, 2, 3, 4, 5)
DERIV = (45.0 / 60.0, -9.0 / 60.0, 1.0 / 60.0)


def decay_of(stiffness):
    half = 0.5 / math.sqrt(stiffness)
    return math.exp(-2.0 * math.asinh(half)), 1.0 / math.sqrt(1.0 + 4.0 * stiffness)


def fields_of(a, b):
    return (
        a[0],
        a[1],
        a[2],
        a[0] * b[0],
        a[0] * b[1],
        a[0] * b[2],
        a[1] * b[1],
        a[1] * b[2],
        a[2] * b[2],
    )


def by_row(index, values):
    out = jnp.full(index.shape, values[0], F32)
    for i, value in enumerate(values[1:], 1):
        out = jnp.where(index == i, F32(value), out)
    return out


def vertical(center, halo, rows):
    total = None
    for k, coef in enumerate(DERIV, 1):
        upper = [
            pltpu.roll(jnp.where(rows >= k, c, h), 8 - k, 0) for c, h in zip(center, halo)
        ]
        lower = [
            pltpu.roll(jnp.where(rows < 8 - k, c, h), k, 0) for c, h in zip(center, halo)
        ]
        above = fields_of([F32(coef) * a for a in upper], upper)
        below = fields_of([F32(coef) * b for b in lower], lower)
        term = [a - b for a, b in zip(above, below)]
        total = term if total is None else [t + s for t, s in zip(total, term)]
    return total


def exchange_kernel(
    decay,
    scale,
    cells,
    blocks,
    v_hbm,
    local_ref,
    deriv_ref,
    carry_ref,
    v_ref,
    halo_ref,
    sums_ref,
    group_ref,
    total_ref,
    ring_ref,
    scan_ref,
    back_ref,
    load_sem,
    halo_send,
    halo_recv,
    send_sem,
    recv_sem,
    group_go,
    y_go,
    z_go,
):
    me = lax.axis_index("gx")
    y = lax.axis_index("gz")
    y_parts = lax.axis_size("gz")
    ring = blocks // GROUP
    z = me // GROUP
    p = lax.rem(me, GROUP)
    above_id = lax.rem(y + 1, y_parts)
    below_id = lax.rem(y + y_parts - 1, y_parts)
    wide = cells // CHUNKS
    rho = decay**cells
    jump = rho**GROUP

    def signal(sem, **device):
        pl.semaphore_signal(sem, inc=1, device_id=device, device_id_type=MESH)

    def in_group(k):
        return lax.rem(p + k, GROUP)

    def group_peer(k):
        return z * GROUP + in_group(k)

    def ring_peer(k):
        return lax.rem(z + k, ring) * GROUP + p

    barrier = pltpu.get_barrier_semaphore()
    even = lax.rem(p, 2) == 0
    for k in range(1, GROUP):

        @pl.when(lax.rem(p + k, 2) == 0)
        def _(k=k):
            signal(barrier, gx=group_peer(k))

    third_chip = p // 2 == 2
    for other in (above_id, below_id):

        @pl.when(third_chip)
        def _(other=other):
            signal(barrier, gx=z * GROUP + 7, gz=other)

        @pl.when(jnp.logical_not(third_chip))
        def _(other=other):
            signal(barrier, gx=me + 1 - lax.rem(p, 2), gz=other)

    def load(n):
        part = pl.ds(n * (cells // LOADS), cells // LOADS)
        return pltpu.make_async_copy(v_hbm.at[:, part], v_ref.at[:, part], load_sem.at[n])

    for n in range(LOADS):
        load(n).start()

    def halo(n, side):
        first, target = ((0, below_id), (8 - HALO, above_id))[side]
        part = pl.ds(sum(PARTS[:n]), PARTS[n])
        layers = pl.ds(first, HALO)
        return pltpu.make_async_remote_copy(
            src_ref=v_hbm.at[:, part, layers],
            dst_ref=halo_ref.at[:, part, layers],
            send_sem=halo_send,
            recv_sem=halo_recv.at[n],
            device_id={"gz": target},
            device_id_type=MESH,
        )

    def both_halos(part, received):
        layers = pl.ds(0, 2 * HALO)
        return pltpu.make_async_remote_copy(
            src_ref=v_hbm.at[:, part, layers],
            dst_ref=halo_ref.at[:, part, layers],
            send_sem=halo_send,
            recv_sem=received,
            device_id={"gz": above_id},
            device_id_type=MESH,
        )

    shape = v_ref.shape[2:]
    rows = lax.broadcasted_iota(jnp.int32, shape, 0)
    zero = jnp.zeros(shape, F32)

    def velocity(x):
        return [v_ref[c, x] for c in range(3)]

    def scaled_fields(x):
        v = velocity(x)
        return fields_of([F32(scale) * a for a in v], v)

    def forward(n, state):
        ahead, back, weight = state
        for u in range(wide):
            x = n * wide + u
            f = scaled_fields(x)
            ahead = [F32(decay) * a + b for a, b in zip(ahead, f)]
            back = [a + weight * b for a, b in zip(back, f)]
            weight = weight * F32(decay)
            for i in range(9):
                local_ref[i, x] = ahead[i]
        return tuple(ahead), tuple(back), weight

    def pass_on():
        pl.semaphore_wait(barrier, GROUP - 1)
        signal(group_go, gx=me + 1)

    pl.when(jnp.logical_and(even, p >= GROUP // 2))(pass_on)

    state = ((zero,) * 9, (zero,) * 9, jnp.ones(shape, F32))
    each = CHUNKS // LOADS
    for n in range(LOADS):
        load(n).wait()
        state = lax.fori_loop(n * each, (n + 1) * each, forward, state)
    for i in range(9):
        sums_ref[i] = state[0][i]
        sums_ref[9 + i] = state[1][i]

    def carries(stage, source, target, source_rows, target_rows, peer):
        return pltpu.make_async_remote_copy(
            src_ref=source.at[:, source_rows],
            dst_ref=target.at[:, target_rows],
            send_sem=send_sem.at[stage],
            recv_sem=recv_sem.at[stage],
            device_id={"gx": peer},
            device_id_type=MESH,
        )

    def all_carries(stage, source, target, count):
        every = pl.ds(0, count - 1)
        return carries(stage, source, target, every, every, me)

    def others(own, order, act):
        for to in order:

            @pl.when(own != to)
            def _(to=to):
                act(to)

    def start_group(stage, source, target, order):
        def start(to):
            peer = z * GROUP + to
            carries(stage, source, target, pl.ds(to, 1), pl.ds(p, 1), peer).start()

        others(p, order, start)

    first = all_carries(0, sums_ref, group_ref, GROUP)
    second = all_carries(1, total_ref, ring_ref, ring)
    third = all_carries(2, scan_ref, back_ref, GROUP)

    pl.when(jnp.logical_and(even, p < GROUP // 2))(pass_on)

    @pl.when(jnp.logical_not(even))
    def _():
        pl.semaphore_wait(group_go, 1)

    @pl.when(p == 4)
    def _():
        for k in range(1, ring):
            signal(barrier, gx=ring_peer(k) + 1)

    start_group(0, sums_ref, group_ref, ORDER1)

    @pl.when(p == 7)
    def _():
        pl.semaphore_wait(barrier, 8)
        for target in (me - 1, me - 2, me - 3):
            signal(y_go, gx=target)

    @pl.when(jnp.logical_and(jnp.logical_not(even), p < 5))
    def _():
        pl.semaphore_wait(barrier, 4)
        signal(y_go, gx=me - 1)

    @pl.when(jnp.logical_or(even, p == 5))
    def _():
        pl.semaphore_wait(y_go, 1)

    for n in range(len(PARTS)):
        for side in range(2):
            halo(n, side).start()

    def backward(n, behind):
        for u in range(wide):
            x = cells - 1 - (n * wide + u)
            for i in range(9):
                local_ref[i, x] = local_ref[i, x] + behind[i]
            f = scaled_fields(x)
            behind = [F32(decay) * (a + b) for a, b in zip(behind, f)]
        return tuple(behind)

    @pl.when(p == 5)
    def _():
        pl.semaphore_wait(barrier, ring - 1)
        for k in range(1, GROUP):
            signal(z_go, gx=group_peer(k))

    def derive(n):
        start = sum(PARTS[:n])
        both_halos(pl.ds(start, PARTS[n]), halo_recv.at[n]).wait_recv()

        def one(j, _):
            x = start + j
            out = vertical(velocity(x), [halo_ref[c, x] for c in range(3)], rows)
            for i in range(9):
                deriv_ref[i, x] = out[i]
            return 0

        lax.fori_loop(0, PARTS[n], one, 0)

    rising = by_row(rows, [rho**b for b in range(GROUP)])
    sinking = by_row(rows, [rho ** (GROUP - 1 - b) for b in range(GROUP)])
    mine = rows == p
    first.wait_recv()
    for i in range(18):
        held = jnp.where(mine, sums_ref[i], group_ref[i])
        group_ref[i] = held
        part = held * (sinking if i < 9 else rising)
        total_ref[i] = jnp.broadcast_to(jnp.sum(part, axis=0, keepdims=True), shape)

    @pl.when(p != 5)
    def _():
        pl.semaphore_wait(z_go, 1)

    def start_ring(*planes):
        def start(to):
            peer = to * GROUP + p
            carries(1, total_ref, ring_ref, pl.ds(z, 1), pl.ds(z, 1), peer).start()

        others(z, planes, start)

    start_ring(0)
    for i in range(18):
        if i < 9:
            run = jnp.where(rows >= 1, pltpu.roll(group_ref[i], 1, 0), F32(0))
            for s in (1, 2, 4):
                moved = jnp.where(rows >= s, pltpu.roll(run, s, 0), F32(0))
                run = run + F32(rho**s) * moved
        else:
            run = jnp.where(rows < 7, pltpu.roll(group_ref[i], 7, 0), F32(0))
            for s in (1, 2, 4):
                moved = jnp.where(rows < 8 - s, pltpu.roll(run, 8 - s, 0), F32(0))
                run = run + F32(rho**s) * moved
        scan_ref[i] = run

    start_ring(1)
    half = CHUNKS // 2
    behind = lax.fori_loop(0, half, backward, (zero,) * 9)
    start_ring(2, 3)
    lax.fori_loop(half, CHUNKS, backward, behind)
    start_ring(*range(4, ring))

    closed = 1.0 / (1.0 - jump**ring)
    powers = [closed * jump**e for e in range(ring)]
    ahead_weight = by_row(lax.rem(z - rows + 2 * ring - 1, ring), powers)
    back_weight = by_row(lax.rem(rows - z + 2 * ring - 1, ring), powers)
    own = rows == z
    second.wait_recv()
    for i in range(18):
        held = jnp.where(own, total_ref[i], ring_ref[i])
        part = held * (ahead_weight if i < 9 else back_weight)
        entering = jnp.broadcast_to(jnp.sum(part, axis=0, keepdims=True), shape)
        scan_ref[i] = scan_ref[i] + (rising if i < 9 else sinking) * entering

    start_group(2, scan_ref, back_ref, ORDER3)

    for n in range(len(PARTS)):
        derive(n)

    third.wait_recv()
    for i in range(18):
        carry_ref[i] = jnp.where(mine, scan_ref[i], back_ref[i])

    for copy in (first, second, third):
        copy.wait_send()
    both_halos(pl.ds(0, cells), halo_recv.at[0]).wait_send()


def write_kernel(decay, cells, local_ref, deriv_ref, carry_ref, out_s, out_d, held, sem_s, sem_d):
    wide = cells // PIECES

    def put_d(n):
        part = pl.ds(n * wide, wide)
        return pltpu.make_async_copy(deriv_ref.at[:, part], out_d.at[:, part], sem_d)

    def put_s(n):
        part = pl.ds(n * wide, wide)
        return pltpu.make_async_copy(held.at[:, part], out_s.at[:, part], sem_s)

    for n in range(PIECES):
        put_d(n).start()

    def correct(n, weights):
        rising, falling = weights
        for u in range(wide):
            x = n * wide + u
            up = rising * F32(decay ** (u + 1))
            down = falling * F32(decay ** (wide - u))
            for i in range(9):
                held[i, x] = local_ref[i, x] + (up * carry_ref[i] + down * carry_ref[9 + i])
        put_s(n).start()
        return rising * F32(decay**wide), falling * F32(decay**-wide)

    shape = carry_ref.shape[1:]
    ones = jnp.ones(shape, F32)
    lax.fori_loop(0, PIECES, correct, (ones, ones * F32(decay ** (cells - wide))))
    pltpu.make_async_copy(deriv_ref, out_d, sem_d).wait()
    pltpu.make_async_copy(held, out_s, sem_s).wait()


def shards(velocity):
    comps, cells, layers, span = velocity.shape
    blocks = lax.axis_size("gx")
    ring = blocks // GROUP
    decay, scale = decay_of((cells * blocks / 8.0) ** 2)
    big = (9, cells, layers, span)
    small = (18, layers, span)
    local, deriv, carry = pl.pallas_call(
        functools.partial(exchange_kernel, decay, scale, cells, blocks),
        out_shape=(
            pltpu.VMEM(big, F32),
            pltpu.VMEM(big, F32),
            pltpu.VMEM(small, F32),
        ),
        in_specs=[pl.BlockSpec(memory_space=pl.ANY)],
        out_specs=[pl.BlockSpec(memory_space=pltpu.VMEM)] * 3,
        scratch_shapes=[
            pltpu.VMEM((comps, cells, layers, span), F32),
            pltpu.VMEM((comps, cells, layers, span), F32),
        ]
        + [pltpu.VMEM(small, F32)] * 6
        + [
            pltpu.SemaphoreType.DMA((LOADS,)),
            pltpu.SemaphoreType.DMA,
            pltpu.SemaphoreType.DMA((len(PARTS),)),
            pltpu.SemaphoreType.DMA((3,)),
            pltpu.SemaphoreType.DMA((3,)),
            pltpu.SemaphoreType.REGULAR,
            pltpu.SemaphoreType.REGULAR,
            pltpu.SemaphoreType.REGULAR,
        ],
        compiler_params=pltpu.CompilerParams(
            collective_id=0, has_side_effects=True, vmem_limit_bytes=44 << 20
        ),
        name="exchange",
    )(velocity)
    return pl.pallas_call(
        functools.partial(write_kernel, decay, cells),
        out_shape=(jax.ShapeDtypeStruct(big, F32), jax.ShapeDtypeStruct(big, F32)),
        in_specs=[pl.BlockSpec(memory_space=pltpu.VMEM)] * 3,
        out_specs=[pl.BlockSpec(memory_space=pltpu.HBM)] * 2,
        scratch_shapes=[
            pltpu.VMEM(big, F32),
            pltpu.SemaphoreType.DMA,
            pltpu.SemaphoreType.DMA,
        ],
        compiler_params=pltpu.CompilerParams(vmem_limit_bytes=24 << 20),
        name="write",
    )(local, deriv, carry)


def solution(mesh):
    spec = P(None, "gx", "gz", None)
    return jax.shard_map(
        shards, mesh=mesh, in_specs=(spec,), out_specs=(spec, spec), check_vma=False
    )
```
